128 devices in a mesh: los: 8 (over z, core), spec: 16 (over x, y).
Axes of the slice: x: 4, y: 4, z: 4, core: 2. Of those that a mesh axis runs over, the one named last changes fastest.
Arguments:
- abundances: bfloat16 [30, 524288], P(None, ('los', 'spec')), may hold values from 0.049804688 to 1
- sightline: int32 [524288], P(('los', 'spec')), may hold values from 0 to 255
- pixel: int32 [524288], P(('los', 'spec')), may hold values from 0 to 255
- counts: int32 [128, 128], P(('los', 'spec')), may hold values from 1 to 32, as said below
- ion_table: float32 [30, 32], replicated, may hold values from 0 to 0.067
- doppler: float32 [32], replicated, may hold values from 2 to 16
- lorentz_share: float32 [32], replicated, may hold values from 0.1 to 0.9
Outputs:
- depth: float32 [32, 2048, 4096], P(None, 'los', 'spec')
The draws below stay inside these ranges and needn't reach their ends.
Inputs may be any that keep to these rules, and one draw needn't show every extreme that they name: `counts`: every source domain has exactly 32 live slots for at least one destination.
All inputs are finite; a program needn't handle non-finite values.
Results may differ from the reference program's by a relative error of at most 0.0024.
Values may be sent and summed in bfloat16 or wider, within the bound.
No kernel may reach another device: no remote copies, remote signals or barrier semaphores. Data moves between devices by JAX's collectives and lax.ppermute only.
A program may use at most 128 MiB of HBM per device.

```python
import math
import jax
import jax.numpy as jnp
from jax import lax

ELEM = 30
ION = 32
PIXELS = 4096
HW = 64
SL_DEV = 256
CAP = 32
PIX_DEV = 256
SIGHTLINES = 2048
PART = 524288
N_SPEC = 16
DEVICES = 128


def draw_counts(key, part):
    key = jax.random.fold_in(key, 7)
    first, second, third = jax.random.split(key, 3)
    raw = jax.random.randint(first, (DEVICES, DEVICES), 1, CAP + 1)
    load = jax.random.randint(second, (1, DEVICES), 1, 5)
    values = jnp.maximum(1, raw * load // 4)
    order = jax.random.permutation(third, DEVICES)
    filled = jnp.arange(DEVICES)[None, :] == order[:, None]
    return jnp.where(filled, CAP, values).astype(jnp.int32)


def plant(values, own_key, low, largest):
    index_at = [jax.random.randint(jax.random.fold_in(own_key, axis), (), 0, length) for axis, length in enumerate(values.shape)]
    widest = values.shape.index(max(values.shape))
    neighbour = index_at[:widest] + [(index_at[widest] + 1) % values.shape[widest]] + index_at[widest + 1:]
    return values.at[tuple(index_at)].set(low).at[tuple(neighbour)].set(largest)


def block_scale(own_key, shape, shards, low, largest):
    def one(dim, blocks):
        heights = jax.random.uniform(jax.random.fold_in(jax.random.fold_in(own_key, 6), dim), (blocks,), jnp.float32, low / len(shards), largest / len(shards))
        return jnp.repeat(jnp.exp(heights), shape[dim] // blocks).reshape((-1,) + (1,) * (len(shape) - dim - 1))

    gain = one(*shards[0])
    for cut in shards[1:]:
        gain = gain * one(*cut)
    return gain


def setup_inputs(seed: int = 0) -> dict:
    seeds = jax.random.split(jax.random.key(seed), 8)
    abundances = jnp.clip(jnp.exp(math.log(1.0) - 2.9996462 * jax.random.uniform(seeds[0], (ELEM, PART), jnp.float32) ** block_scale(seeds[0], (ELEM, PART), ((1, 128),), -0.2, 0.2)), 0.049804688, 1.0).astype(jnp.bfloat16)
    sightline = plant(jax.random.randint(seeds[1], (PART,), 0, SL_DEV), jax.random.fold_in(seeds[1], 1), 0, SL_DEV - 1).astype(jnp.int32)
    pixel = plant(jax.random.randint(seeds[2], (PART,), 0, PIX_DEV), jax.random.fold_in(seeds[2], 1), 0, PIX_DEV - 1).astype(jnp.int32)
    counts = draw_counts(jax.random.fold_in(seeds[7], 71), 0)
    ion_table = jnp.clip(jax.random.uniform(seeds[4], (ELEM, ION), jnp.float32, 0.0, 0.067), 0.0, 0.067)
    doppler = jnp.clip(jnp.exp(jax.random.uniform(seeds[5], (ION,), jnp.float32, math.log(2.0), math.log(16.0))), 2.0, 16.0)
    lorentz_share = jnp.clip(jax.random.uniform(seeds[6], (ION,), jnp.float32, 0.1, 0.9), 0.1, 0.9)
    return {"abundances": abundances, "sightline": sightline, "pixel": pixel, "counts": counts, "ion_table": ion_table, "doppler": doppler, "lorentz_share": lorentz_share}


def line_shape(offset, doppler, share):
    u = offset / doppler
    return (1.0 - share) * jnp.exp(-u * u) + share / (1.0 + u * u)


def reference(abundances, sightline, pixel, counts, ion_table, doppler, lorentz_share):
    index = jnp.arange(PART, dtype=jnp.int32)
    source = index // (DEVICES * CAP)
    target = (index // CAP) % DEVICES
    position = index % CAP
    live = position < counts[source, target]
    columns = jnp.dot(ion_table.T, abundances.astype(jnp.float32), precision=lax.Precision.HIGHEST)
    columns = jnp.where(live[None, :], columns, 0.0).astype(jnp.bfloat16)
    glob_line = (target // N_SPEC) * SL_DEV + sightline
    glob_pixel = (target % N_SPEC) * PIX_DEV + pixel
    cell = (glob_line * PIXELS + glob_pixel).astype(jnp.int32)
    grid = jnp.zeros((ION, SIGHTLINES * PIXELS), jnp.float32)
    grid = grid.at[:, cell].add(columns.astype(jnp.float32))
    grid = grid.reshape(ION, SIGHTLINES, PIXELS)
    offsets = jnp.arange(-HW, HW + 1).astype(jnp.float32)
    steps_all = jnp.arange(PIXELS)
    signed = jnp.where(steps_all <= PIXELS // 2, steps_all, steps_all - PIXELS).astype(jnp.float32)

    def one_ion(args):
        plane, width, share = args
        total = jnp.sum(line_shape(offsets, width, share))
        kernel = jnp.where(jnp.abs(signed) <= HW, line_shape(signed, width, share), 0.0) / total
        spectrum = jnp.fft.rfft(plane, axis=1) * jnp.fft.rfft(kernel)[None, :]
        return jnp.fft.irfft(spectrum, n=PIXELS, axis=1).astype(plane.dtype)

    return lax.map(one_ion, (grid, doppler, lorentz_share))
```

```python
import jax
import jax.numpy as jnp
from jax import lax
from jax.experimental import pallas as pl
from jax.experimental.pallas import tpu as pltpu
from jax.sharding import PartitionSpec as P

ELEM = 30
ION = 32
VAL = 32
HW = 64
SL_DEV = 256
PIX_DEV = 256
CAP = 32
DEAD = 256.0
LISTS = 3
GROUP = 256
SUPER = 768
BUCKETS = 6
BF = jnp.bfloat16
F32 = jnp.float32


def swap_blocks(tiles):
    lane = lax.broadcasted_iota(jnp.int32, (8, 128), 1)
    low = lane < 64
    even = (lane // 32) % 2 == 0
    far = [pltpu.roll(t, 64, 1) for t in tiles]
    half = [
        jnp.where(low, tiles[0], far[2]),
        jnp.where(low, tiles[1], far[3]),
        jnp.where(low, far[0], tiles[2]),
        jnp.where(low, far[1], tiles[3]),
    ]
    out = [None] * 4
    for p in (0, 2):
        a, b = half[p], half[p + 1]
        out[p] = jnp.where(even, a, pltpu.roll(b, 32, 1))
        out[p + 1] = jnp.where(even, pltpu.roll(a, 96, 1), b)
    return out


def pack_kernel(abund_ref, line_ref, pixel_ref, counts_ref, out_ref, *, n_spec):
    devices = counts_ref.shape[1]
    quads = devices // 4
    row = lax.broadcasted_iota(jnp.int32, (quads, devices), 0)
    col = lax.broadcasted_iota(jnp.int32, (quads, devices), 1)
    spread = jnp.where(col // 4 == row, counts_ref[...].astype(F32), 0.0).astype(BF)
    inner = lax.broadcasted_iota(jnp.int32, (devices, 128), 0)
    outer = lax.broadcasted_iota(jnp.int32, (devices, 128), 1)
    pick = jnp.where(inner % 4 == outer // CAP, 1.0, 0.0).astype(BF)
    live_count = jnp.dot(spread, pick, preferred_element_type=F32)
    slot = (lax.broadcasted_iota(jnp.int32, (quads, 128), 1) % CAP).astype(F32)
    line = jnp.where(slot < live_count, line_ref[...].astype(F32), DEAD)
    pixel = pixel_ref[...].astype(F32)
    for t in range(devices // n_spec):
        msgs = []
        for a in range(t * n_spec // 4, (t + 1) * n_spec // 4):
            ab = abund_ref[:, a * 128 : (a + 1) * 128].astype(F32)
            vals = jnp.concatenate([ab, line[a : a + 1], pixel[a : a + 1]], axis=0)
            msgs += swap_blocks([vals[8 * j : 8 * j + 8] for j in range(4)])
        for b in range(0, n_spec, 2):
            parts = []
            for c in (b, b + 1):
                parts += [msgs[c], msgs[(c - 1) % n_spec], msgs[(c + 1) % n_spec]]
            out_ref[(t * n_spec + b) // 2] = jnp.concatenate(parts, axis=0).astype(BF)


def profile_kernel(doppler_ref, share_ref, out_ref):
    row = lax.broadcasted_iota(jnp.int32, (4 * HW, 2 * HW), 0)
    col = lax.broadcasted_iota(jnp.int32, (4 * HW, 2 * HW), 1)

    def table(i, offset):
        share = share_ref[i]
        width = doppler_ref[i]
        near = jnp.abs(offset) <= HW
        u = offset.astype(F32) / width
        raw = (1.0 - share) * jnp.exp(-u * u) + share / (1.0 + u * u)
        raw = jnp.where(near, raw, 0.0)
        return raw / jnp.sum(raw, axis=0, keepdims=True)

    def body(k, carry):
        out_ref[2 * k] = table(2 * k, col + HW - row).astype(BF)
        out_ref[2 * k + 1] = table(2 * k + 1, col + HW - (row ^ HW)).astype(BF)
        return carry

    lax.fori_loop(0, ION // 2, body, 0)


def nt(a, b):
    return lax.dot_general(a, b, (((1,), (1,)), ((), ())), preferred_element_type=F32)


def sort_slots(recv_ref, rec_ref, line_ref, pixel_ref, pos_ref, cnt_ref, sorted_ref, groups):
    per = groups // LISTS

    def unpack(g, carry):
        tiles = []
        for p in range(4):
            block = recv_ref[g * 4 + p].astype(F32)
            tiles.append([block[8 * m : 8 * m + 8] for m in range(6)])
        for kind in range(LISTS):
            halves = []
            for h in range(2):
                srcs = [tiles[2 * h + s // 2][3 * (s % 2) + kind] for s in range(4)]
                halves.append(jnp.concatenate(swap_blocks(srcs), axis=0))
            rec = jnp.concatenate(halves, axis=1)
            rec_ref[kind * per + g] = rec.astype(BF)
            line_ref[pl.ds(kind * per + g, 1), :] = rec[ELEM : ELEM + 1]
            pixel_ref[pl.ds(kind * per + g, 1), :] = rec[ELEM + 1 : ELEM + 2]
        return carry

    lax.fori_loop(0, per, unpack, 0)

    live = line_ref[...] < SL_DEV
    block = jnp.floor(pixel_ref[...] * (1.0 / HW))
    own_live, own_block = live[:per], block[:per]
    marks = [jnp.where(own_live & (own_block == b), 1.0, 0.0) for b in range(4)]
    marks.append(jnp.where(live[per : 2 * per] & (block[per : 2 * per] == 3.0), 1.0, 0.0))
    marks.append(jnp.where(live[2 * per :] & (block[2 * per :] == 0.0), 1.0, 0.0))
    marks = jnp.concatenate(marks, axis=0).astype(BF)
    before = lax.broadcasted_iota(jnp.int32, (GROUP, GROUP), 0)
    after = lax.broadcasted_iota(jnp.int32, (GROUP, GROUP), 1)
    rank = jnp.dot(marks, (before < after).astype(F32).astype(BF), preferred_element_type=F32)
    total = jnp.dot(marks, jnp.ones((GROUP, GROUP), BF), preferred_element_type=F32)
    cnt_ref[...] = nt(jnp.ones((8, GROUP), BF), marks).astype(jnp.int32)
    marks = marks.astype(F32)
    part = lambda x, b: x[b * per : (b + 1) * per]
    start = jnp.zeros((per, GROUP), F32)
    own = jnp.zeros((per, GROUP), F32)
    for b in range(4):
        own = own + part(marks, b) * (start + part(rank, b))
        start = start + part(total, b)
    any_own = part(marks, 0) + part(marks, 1) + part(marks, 2) + part(marks, 3)
    pos_ref[:per] = jnp.where(any_own > 0, own, 2.0 * GROUP)
    for kind in (1, 2):
        used = part(marks, 3 + kind)
        pos_ref[kind * per : (kind + 1) * per] = jnp.where(used > 0, part(rank, 3 + kind), 2.0 * GROUP)

    target = lax.broadcasted_iota(jnp.int32, (GROUP, GROUP), 0).astype(F32)

    def permute(g, carry):
        pos = pos_ref[pl.ds(g, 1), :]
        perm = jnp.where(pos == target, 1.0, 0.0).astype(BF)
        sorted_ref[g, :GROUP] = nt(perm, rec_ref[g])
        return carry

    lax.fori_loop(0, groups, permute, 0)


def gather_buckets(smem_cnt, first_ref, sorted_ref, rows_ref, groups):
    per = groups // LISTS
    lane = lax.broadcasted_iota(jnp.int32, (32, VAL), 1)
    dead = jnp.where(lane == ELEM, DEAD, 0.0).astype(F32)
    plan = [(1, 4, ()), (0, 0, ()), (0, 1, (0,)), (0, 2, (0, 1)), (0, 3, (0, 1, 2)), (2, 5, ())]
    first = jnp.int32(0)
    for b, (kind, mark, smaller) in enumerate(plan):
        first_ref[b] = first
        base = first * SUPER
        total = lax.fori_loop(0, per, lambda g, s: s + smem_cnt[0, mark * per + g], jnp.int32(0))
        supers = jnp.maximum((total + SUPER - 1) // SUPER, 1)

        def fill(k, carry):
            rows_ref[pl.ds(pl.multiple_of(base + k * 32, 32), 32), :] = dead
            return carry

        lax.fori_loop(total // 32, supers * (SUPER // 32), fill, 0)

        def move(g, off):
            count = smem_cnt[0, mark * per + g]
            src = jnp.int32(0)
            for m in smaller:
                src = src + smem_cnt[0, m * per + g]

            def chunk(k, carry):
                rows_ref[pl.ds(off + k * 32, 32), :] = sorted_ref[kind * per + g, pl.ds(src + k * 32, 32), :]
                return carry

            lax.fori_loop(0, (count + 31) // 32, chunk, 0)
            return off + count

        end = lax.fori_loop(0, per, move, base)
        rows_ref[pl.ds(end, 32), :] = dead
        first = first + supers
    first_ref[BUCKETS] = first


def make_columns(first_ref, table_ref, rows_ref, col_ref, linehot_ref, pixhot_ref):
    table = table_ref[...]
    hi = table.astype(BF)
    rest = table - hi.astype(F32)
    mid = rest.astype(BF)
    low = (rest - mid.astype(F32)).astype(BF)
    row = lax.broadcasted_iota(jnp.int32, (16, VAL), 0)
    lane = lax.broadcasted_iota(jnp.int32, (16, VAL), 1)
    picks = jnp.where(lane == row + ELEM, 1.0, 0.0).astype(BF)
    left = jnp.concatenate([hi, mid, low, picks], axis=0)
    lines = lax.broadcasted_iota(jnp.int32, (SL_DEV, SUPER), 0).astype(F32)
    pixels = lax.broadcasted_iota(jnp.int32, (HW, SUPER), 0).astype(F32)

    def one(s, carry):
        rows = rows_ref[pl.ds(pl.multiple_of(s * SUPER, SUPER), SUPER), :].astype(BF)
        got = nt(left, rows)
        cols = got[:ION] + got[ION : 2 * ION] + got[2 * ION : 3 * ION]
        for i in range(ION):
            col_ref[s, i] = jnp.broadcast_to(cols[i : i + 1], (16, SUPER)).astype(BF)
        line = got[3 * ION : 3 * ION + 1]
        pixel = got[3 * ION + 1 : 3 * ION + 2]
        pixel = pixel - HW * jnp.floor(pixel * (1.0 / HW))
        linehot_ref[s] = jnp.where(line == lines, 1.0, 0.0).astype(BF)
        pixhot_ref[s] = jnp.where(pixel == pixels, 1.0, 0.0).astype(BF)
        return carry

    lax.fori_loop(0, first_ref[BUCKETS], one, 0)


def main_kernel(recv_ref, table_ref, prof_ref, out_ref, rec_ref, line_ref, pixel_ref, pos_ref, cnt_ref,
                sorted_ref, rows_ref, col_ref, linehot_ref, pixhot_ref, acc_ref, smem_cnt, first_ref, sem):
    groups = rec_ref.shape[0]
    quad = pl.program_id(0)

    @pl.when(quad == 0)
    def _():
        sort_slots(recv_ref, rec_ref, line_ref, pixel_ref, pos_ref, cnt_ref, sorted_ref, groups)
        copy = pltpu.make_async_copy(cnt_ref, smem_cnt, sem)
        copy.start()
        copy.wait()
        gather_buckets(smem_cnt, first_ref, sorted_ref, rows_ref, groups)
        make_columns(first_ref, table_ref, rows_ref, col_ref, linehot_ref, pixhot_ref)

    def product(s, odd):
        hot = pixhot_ref[s]
        parts = []
        for j in range(4):
            col = col_ref[s, quad * 4 + (j ^ 1 if odd else j)]
            parts.append(hot * jnp.concatenate([col] * (HW // 16), axis=0))
        return nt(linehot_ref[s], jnp.concatenate(parts, axis=0))

    for b in range(BUCKETS):
        start = first_ref[b]
        acc_ref[b] = product(start, b % 2)

        def more(s, carry):
            acc_ref[b] += product(s, b % 2)
            return carry

        lax.fori_loop(start + 1, first_ref[b + 1], more, 0)

    low = lax.broadcasted_iota(jnp.int32, (SL_DEV, 128), 1) < HW
    for j in range(4):
        half = pl.ds(128 * (j // 2), 128)
        parts = []
        for b in range(0, BUCKETS, 2):
            x, y = acc_ref[b, :, half], acc_ref[b + 1, :, half]
            parts.append((jnp.where(low, y, x) if j % 2 else jnp.where(low, x, y)).astype(BF))
        prof = prof_ref[j]
        for c in range(2):
            lhs = jnp.concatenate(parts[c : c + 2], axis=1)
            out_ref[j, :, 128 * c : 128 * c + 128] = jnp.dot(lhs, prof, preferred_element_type=F32)


def on_device(abundances, sightline, pixel, counts, ion_table, doppler, lorentz_share):
    n_spec = lax.axis_size("spec")
    devices = lax.axis_size("los") * n_spec
    n_slots = abundances.shape[1]
    vmem = pl.BlockSpec(memory_space=pltpu.VMEM)
    smem = pl.BlockSpec(memory_space=pltpu.SMEM)
    sent = pl.pallas_call(
        lambda *refs: pack_kernel(*refs, n_spec=n_spec),
        out_shape=jax.ShapeDtypeStruct((devices // 2, 2 * LISTS * 8, 128), BF),
        in_specs=[vmem] * 4,
        out_specs=vmem,
        compiler_params=pltpu.CompilerParams(vmem_limit_bytes=32 * 2**20),
        name="pack",
    )(abundances, sightline.reshape(n_slots // 128, 128), pixel.reshape(n_slots // 128, 128), counts)
    prof = pl.pallas_call(
        profile_kernel,
        out_shape=jax.ShapeDtypeStruct((ION, 4 * HW, 2 * HW), BF),
        in_specs=[smem] * 2,
        out_specs=vmem,
        compiler_params=pltpu.CompilerParams(vmem_limit_bytes=16 * 2**20),
        cost_estimate=pl.CostEstimate(flops=20_000_000, bytes_accessed=2 * 2**20, transcendentals=3_000_000),
        name="profile",
    )(doppler, lorentz_share)
    table = jnp.pad(ion_table.T, ((0, 0), (0, VAL - ELEM)))
    got = lax.all_to_all(
        sent.reshape(devices, LISTS * 8, 128), ("los", "spec"), split_axis=0, concat_axis=0, tiled=True
    ).reshape(devices // 2, 2 * LISTS * 8, 128)

    groups = LISTS * n_slots // GROUP
    supers = -(-LISTS * n_slots // SUPER) + BUCKETS
    return pl.pallas_call(
        main_kernel,
        grid=(ION // 4,),
        out_shape=jax.ShapeDtypeStruct((ION, SL_DEV, PIX_DEV), F32),
        in_specs=[
            vmem,
            vmem,
            pl.BlockSpec((4, 4 * HW, 2 * HW), lambda q: (q, 0, 0)),
        ],
        out_specs=pl.BlockSpec((4, SL_DEV, PIX_DEV), lambda q: (q, 0, 0)),
        scratch_shapes=[
            pltpu.VMEM((groups, VAL, GROUP), BF),
            pltpu.VMEM((groups, GROUP), F32),
            pltpu.VMEM((groups, GROUP), F32),
            pltpu.VMEM((groups, GROUP), F32),
            pltpu.VMEM((8, 2 * groups), jnp.int32),
            pltpu.VMEM((groups, GROUP + 32, VAL), F32),
            pltpu.VMEM((supers * SUPER + 64, VAL), F32),
            pltpu.VMEM((supers, ION, 16, SUPER), BF),
            pltpu.VMEM((supers, SL_DEV, SUPER), BF),
            pltpu.VMEM((supers, HW, SUPER), BF),
            pltpu.VMEM((BUCKETS, SL_DEV, 4 * HW), F32),
            pltpu.SMEM((8, 2 * groups), jnp.int32),
            pltpu.SMEM((BUCKETS + 1,), jnp.int32),
            pltpu.SemaphoreType.DMA,
        ],
        compiler_params=pltpu.CompilerParams(vmem_limit_bytes=60 * 2**20),
        name="deposit_broaden",
    )(got, table, prof)


def solution(mesh):
    in_specs = (
        P(None, ("los", "spec")),
        P(("los", "spec")),
        P(("los", "spec")),
        P(("los", "spec"), None),
        P(),
        P(),
        P(),
    )
    return jax.shard_map(
        on_device, mesh=mesh, in_specs=in_specs, out_specs=P(None, "los", "spec"), check_vma=False
    )
```

```python
import jax
import jax.numpy as jnp
from jax import lax
from jax.experimental import pallas as pl
from jax.experimental.pallas import tpu as pltpu
from jax.sharding import PartitionSpec as P

ELEM = 30
ION = 32
VAL = 32
HW = 64
SL_DEV = 256
PIX_DEV = 256
CAP = 32
DEAD = 256.0
NOWHERE = 512.0
LISTS = 3
GROUP = 256
SUPER = 256
PX = 16
SIDE = HW // PX
OWN = PIX_DEV // PX
BUCKETS = OWN + 2 * SIDE
STEP = 24
PITCH = GROUP + STEP
BF = jnp.bfloat16
F32 = jnp.float32
I32 = jnp.int32


def iota(shape, dim):
    return lax.broadcasted_iota(I32, shape, dim)


def nt(a, b):
    return lax.dot_general(a, b, (((1,), (1,)), ((), ())), preferred_element_type=F32)


def tn(a, b):
    return lax.dot_general(a, b, (((0,), (0,)), ((), ())), preferred_element_type=F32)


def swap_blocks(tiles):
    lane = iota((8, 128), 1)
    low = lane < 64
    even = (lane // 32) % 2 == 0
    far = [pltpu.roll(t, 64, 1) for t in tiles]
    half = [
        jnp.where(low, tiles[0], far[2]),
        jnp.where(low, tiles[1], far[3]),
        jnp.where(low, far[0], tiles[2]),
        jnp.where(low, far[1], tiles[3]),
    ]
    out = [None] * 4
    for p in (0, 2):
        a, b = half[p], half[p + 1]
        out[p] = jnp.where(even, a, pltpu.roll(b, 32, 1))
        out[p + 1] = jnp.where(even, pltpu.roll(a, 96, 1), b)
    return out


def pack_kernel(abund_hbm, line_hbm, pixel_hbm, counts_hbm, out_ref, abund_ref, line_ref, pixel_ref, counts_ref,
                sems, *, n_spec):
    copies = [
        pltpu.make_async_copy(src, dst, sems.at[k])
        for k, (src, dst) in enumerate(
            ((counts_hbm, counts_ref), (line_hbm, line_ref), (pixel_hbm, pixel_ref), (abund_hbm, abund_ref))
        )
    ]
    for copy in copies:
        copy.start()
    devices = counts_ref.shape[1]
    quads = devices // 4
    row = iota((quads, devices), 0)
    col = iota((quads, devices), 1)
    pick = jnp.where(iota((devices, 128), 0) % 4 == iota((devices, 128), 1) // CAP, 1.0, 0.0).astype(BF)
    slot = (iota((quads, 128), 1) % CAP).astype(F32)
    copies[0].wait()
    spread = jnp.where(col // 4 == row, counts_ref[...].astype(F32), 0.0).astype(BF)
    live_count = jnp.dot(spread, pick, preferred_element_type=F32)
    copies[1].wait()
    line = jnp.where(slot < live_count, line_ref[...].astype(F32), DEAD)
    copies[2].wait()
    pixel = pixel_ref[...].astype(F32)
    copies[3].wait()
    for t in range(devices // n_spec):
        msgs = []
        for a in range(t * n_spec // 4, (t + 1) * n_spec // 4):
            ab = abund_ref[:, a * 128 : (a + 1) * 128].astype(F32)
            vals = jnp.concatenate([ab, line[a : a + 1], pixel[a : a + 1]], axis=0)
            msgs += swap_blocks([vals[8 * j : 8 * j + 8] for j in range(4)])
        for b in range(0, n_spec, 2):
            parts = []
            for c in (b, b + 1):
                parts += [msgs[c], msgs[(c - 1) % n_spec], msgs[(c + 1) % n_spec]]
            out_ref[(t * n_spec + b) // 2] = jnp.concatenate(parts, axis=0).astype(BF)


def prepare_kernel(doppler_ref, share_ref, table_ref, prof_ref, norm_ref, left_ref, scan_ref, first_ref, tri_ref):
    offset = iota((4 * HW, 2 * HW), 1) + HW - iota((4 * HW, 2 * HW), 0)
    near = jnp.abs(offset) <= HW
    offset = offset.astype(F32)

    def body(i, carry):
        share = share_ref[i]
        u = offset / doppler_ref[i]
        raw = (1.0 - share) * jnp.exp(-u * u) + share / (1.0 + u * u)
        raw = jnp.where(near, raw, 0.0)
        prof_ref[i] = raw.astype(BF)
        norm_ref[i] = jnp.broadcast_to(1.0 / jnp.sum(raw, axis=0, keepdims=True), (8, 2 * HW))
        return carry

    lax.fori_loop(0, ION, body, 0)

    table = table_ref[...]
    hi = table.astype(BF)
    rest = table - hi.astype(F32)
    mid = rest.astype(BF)
    low = (rest - mid.astype(F32)).astype(BF)
    picks = jnp.where(iota((16, VAL), 1) == iota((16, VAL), 0) + ELEM, 1.0, 0.0).astype(BF)
    left_ref[...] = jnp.concatenate([hi, mid, low, picks], axis=0)

    n = scan_ref.shape[0]
    per = n // BUCKETS
    x, y = iota((n, n), 0), iota((n, n), 1)
    xb, yb = x // per, y // per
    kind = lambda b: jnp.where(b < SIDE, 1, jnp.where(b < SIDE + OWN, 0, 2))
    one = lambda m: jnp.where(m, 1.0, 0.0).astype(BF)
    scan_ref[:, :n] = one((xb == yb) & (x < y))
    scan_ref[:, n : 2 * n] = one((kind(xb) == kind(yb)) & (x % per == y % per) & (x < y))
    scan_ref[:, 2 * n :] = one(xb == yb)
    first_ref[...] = one((x % per == 0) & (xb < yb))
    tri_ref[...] = one(iota((GROUP, GROUP), 0) < iota((GROUP, GROUP), 1))


def unpack(recv_ref, rec_ref, line_ref, pixel_ref, per):
    def body(g, carry):
        tiles = []
        for p in range(4):
            block = recv_ref[g * 4 + p].astype(F32)
            tiles.append([block[8 * m : 8 * m + 8] for m in range(2 * LISTS)])
        for kind in range(LISTS):
            halves = []
            for h in range(2):
                srcs = [tiles[2 * h + s // 2][LISTS * (s % 2) + kind] for s in range(4)]
                halves.append(jnp.concatenate(swap_blocks(srcs), axis=0))
            rec = jnp.concatenate(halves, axis=1)
            rec_ref[kind * per + g] = rec.astype(BF)
            line_ref[pl.ds(kind * per + g, 1), :] = rec[ELEM : ELEM + 1]
            pixel_ref[pl.ds(kind * per + g, 1), :] = rec[ELEM + 1 : ELEM + 2]
        return carry

    lax.fori_loop(0, per, body, 0, unroll=2)


def rank_slots(line_ref, pixel_ref, scan_ref, first_ref, tri_ref, pos_ref, info_ref, per):
    live = line_ref[...] < SL_DEV
    block = jnp.where(live, jnp.floor(pixel_ref[...] * (1.0 / PX)), -1.0)
    marks = []
    for b in range(BUCKETS):
        if b < SIDE:
            kind, which = 1, OWN - SIDE + b
        elif b < SIDE + OWN:
            kind, which = 0, b - SIDE
        else:
            kind, which = 2, b - SIDE - OWN
        marks.append(jnp.where(block[kind * per : (kind + 1) * per] == which, 1.0, 0.0).astype(BF))
    marks = jnp.concatenate(marks, axis=0)
    n = BUCKETS * per
    rank = jnp.dot(marks, tri_ref[...], preferred_element_type=F32)
    total = jnp.dot(marks, jnp.ones((GROUP, GROUP), BF), preferred_element_type=F32)
    count = nt(jnp.ones((8, GROUP), BF), marks)
    for kind, (lo, hi) in enumerate(((SIDE, SIDE + OWN), (0, SIDE), (SIDE + OWN, BUCKETS))):
        start = jnp.zeros((per, GROUP), F32)
        place = jnp.zeros((per, GROUP), F32)
        used = jnp.zeros((per, GROUP), F32)
        for b in range(lo, hi):
            rows = slice(b * per, (b + 1) * per)
            mark = marks[rows].astype(F32)
            place = place + mark * (start + rank[rows])
            used = used + mark
            start = start + total[rows]
        pos_ref[kind * per : (kind + 1) * per] = jnp.where(used > 0, place, NOWHERE)
    sums = jnp.dot(count.astype(BF), scan_ref[...], preferred_element_type=F32)
    ahead, source, whole = sums[:, :n], sums[:, n : 2 * n], sums[:, 2 * n :]
    supers = jnp.maximum(jnp.floor((whole + (SUPER - 1)) * (1.0 / SUPER)), 1.0)
    first = jnp.dot(supers.astype(BF), first_ref[...], preferred_element_type=F32)
    lane = iota((8, n), 1)
    b = lane // per
    kind = jnp.where(b < SIDE, 1, jnp.where(b < SIDE + OWN, 0, 2))
    base = ((kind * per + lane % per) * PITCH).astype(F32)
    longest = jnp.broadcast_to(jnp.max(count, axis=1, keepdims=True), (8, n))
    row = iota((8, n), 0)
    info = jnp.zeros((8, n), F32)
    for k, value in enumerate((source + base, first * SUPER + ahead, count, first, whole, supers, longest)):
        info = jnp.where(row == k, value, info)
    info_ref[...] = info.astype(I32)


def sort_groups(rec_ref, pos_ref, sorted_ref, groups):
    target = iota((GROUP, GROUP), 0).astype(F32).astype(BF)

    def body(g, carry):
        pos = jnp.broadcast_to(pos_ref[pl.ds(g, 1), :], (16, GROUP)).astype(BF)
        pos = jnp.concatenate([pos] * (GROUP // 16), axis=0)
        perm = jnp.where(pos == target, jnp.ones((), BF), jnp.zeros((), BF))
        sorted_ref[pl.ds(pl.multiple_of(g * PITCH, 8), GROUP), :] = nt(perm, rec_ref[g])
        return carry

    lax.fori_loop(0, groups, body, 0, unroll=4)


def join_runs(info, sorted_ref, rows_ref, n):
    def body(k, carry):
        rows_ref[pl.ds(info[1, k], STEP), :] = sorted_ref[pl.ds(info[0, k], STEP), :]
        return carry

    lax.fori_loop(0, n, body, 0, unroll=16)

    @pl.when(info[6, 0] > STEP)
    def _():
        def tail(k, carry):
            def one(r, c):
                rows_ref[pl.ds(info[1, k] + r, 1), :] = sorted_ref[pl.ds(info[0, k] + r, 1), :]
                return c

            lax.fori_loop(STEP, info[2, k], one, 0)
            return carry

        lax.fori_loop(0, n, tail, 0)


def deposit(info, left_ref, rows_ref, grid_ref, acc_ref, per):
    lane = iota((1, SUPER), 1)
    pixels = iota((PX, SUPER), 0).astype(F32)
    lines = iota((SL_DEV, SUPER), 0).astype(F32).astype(BF)
    one, zero = jnp.ones((), BF), jnp.zeros((), BF)

    def product(s, count):
        rows = rows_ref[pl.ds(pl.multiple_of(s * SUPER, SUPER), SUPER), :].astype(BF)
        got = nt(left_ref[...], rows)
        valid = lane < count
        cols = got[:ION] + got[ION : 2 * ION] + got[2 * ION : 3 * ION]
        cols = jnp.where(valid, cols, 0.0)
        line = jnp.where(valid, got[3 * ION : 3 * ION + 1], DEAD)
        pixel = got[3 * ION + 1 : 3 * ION + 2]
        pixel = pixel - PX * jnp.floor(pixel * (1.0 / PX))
        pixhot = jnp.where(jnp.broadcast_to(pixel, (PX, SUPER)) == pixels, 1.0, 0.0).astype(BF)
        spread = [jnp.broadcast_to(cols[i : i + 1], (PX, SUPER)).astype(BF) * pixhot for i in range(ION)]
        line = jnp.broadcast_to(line, (16, SUPER)).astype(BF)
        line = jnp.concatenate([line] * (SL_DEV // 16), axis=0)
        return nt(jnp.concatenate(spread, axis=0), jnp.where(line == lines, one, zero))

    def store(b, value):
        at = pl.ds(pl.multiple_of(b * PX, PX), PX)
        for i in range(ION):
            grid_ref[i, at, :] = value[i * PX : (i + 1) * PX].astype(BF)

    def body(b, carry):
        store(b, product(info[3, b * per], info[4, b * per]))
        return carry

    lax.fori_loop(0, BUCKETS, body, 0, unroll=2)

    last = (BUCKETS - 1) * per

    @pl.when(info[3, last] + info[5, last] > BUCKETS)
    def _():
        def again(b, carry):
            k = b * per

            @pl.when(info[5, k] > 1)
            def _():
                acc_ref[...] = jnp.zeros_like(acc_ref)

                def more(s, c):
                    acc_ref[...] += product(info[3, k] + s, info[4, k] - s * SUPER)
                    return c

                lax.fori_loop(0, info[5, k], more, 0)
                store(b, acc_ref[...])

            return carry

        lax.fori_loop(0, BUCKETS, again, 0)


def main_kernel(recv_ref, left_ref, scan_ref, first_ref, tri_ref, prof_ref, norm_ref, out_ref, rec_ref, line_ref,
                pixel_ref, pos_ref, info_ref, sorted_ref, rows_ref, grid_ref, acc_ref, info, sem):
    groups = rec_ref.shape[0]
    per = groups // LISTS
    quad = pl.program_id(0)

    @pl.when(quad == 0)
    def _():
        unpack(recv_ref, rec_ref, line_ref, pixel_ref, per)
        rank_slots(line_ref, pixel_ref, scan_ref, first_ref, tri_ref, pos_ref, info_ref, per)
        copy = pltpu.make_async_copy(info_ref, info, sem)
        copy.start()
        sort_groups(rec_ref, pos_ref, sorted_ref, groups)
        copy.wait()
        join_runs(info, sorted_ref, rows_ref, BUCKETS * per)
        deposit(info, left_ref, rows_ref, grid_ref, acc_ref, per)

    for j in range(4):
        plane = grid_ref[quad * 4 + j]
        norm = norm_ref[j, 0:1]
        out_ref[j, :, :128] = tn(plane[:256], prof_ref[j]) * norm
        out_ref[j, :, 128:] = tn(plane[128:], prof_ref[j]) * norm


def on_device(abundances, sightline, pixel, counts, ion_table, doppler, lorentz_share):
    n_spec = lax.axis_size("spec")
    devices = lax.axis_size("los") * n_spec
    n_slots = abundances.shape[1]
    vmem = pl.BlockSpec(memory_space=pltpu.VMEM)
    smem = pl.BlockSpec(memory_space=pltpu.SMEM)
    anywhere = pl.BlockSpec(memory_space=pltpu.HBM)
    sent = pl.pallas_call(
        lambda *refs: pack_kernel(*refs, n_spec=n_spec),
        out_shape=jax.ShapeDtypeStruct((devices // 2, 2 * LISTS * 8, 128), BF),
        in_specs=[anywhere] * 4,
        out_specs=vmem,
        scratch_shapes=[
            pltpu.VMEM(abundances.shape, BF),
            pltpu.VMEM((n_slots // 128, 128), I32),
            pltpu.VMEM((n_slots // 128, 128), I32),
            pltpu.VMEM(counts.shape, I32),
            pltpu.SemaphoreType.DMA((4,)),
        ],
        compiler_params=pltpu.CompilerParams(vmem_limit_bytes=32 * 2**20),
        name="pack",
    )(abundances, sightline.reshape(n_slots // 128, 128), pixel.reshape(n_slots // 128, 128), counts)
    groups = LISTS * n_slots // GROUP
    n = BUCKETS * groups // LISTS
    table = jnp.pad(ion_table.T, ((0, 0), (0, VAL - ELEM)))
    prof, norm, left, scan, first, tri = pl.pallas_call(
        prepare_kernel,
        out_shape=[
            jax.ShapeDtypeStruct((ION, 4 * HW, 2 * HW), BF),
            jax.ShapeDtypeStruct((ION, 8, 2 * HW), F32),
            jax.ShapeDtypeStruct((3 * ION + 16, VAL), BF),
            jax.ShapeDtypeStruct((n, 3 * n), BF),
            jax.ShapeDtypeStruct((n, n), BF),
            jax.ShapeDtypeStruct((GROUP, GROUP), BF),
        ],
        in_specs=[smem, smem, vmem],
        out_specs=[vmem] * 6,
        compiler_params=pltpu.CompilerParams(vmem_limit_bytes=32 * 2**20),
        cost_estimate=pl.CostEstimate(flops=20_000_000, bytes_accessed=4 * 2**20, transcendentals=3_000_000),
        name="prepare",
    )(doppler, lorentz_share, table)
    got = lax.all_to_all(
        sent.reshape(devices, LISTS * 8, 128), ("los", "spec"), split_axis=0, concat_axis=0, tiled=True
    ).reshape(devices // 2, 2 * LISTS * 8, 128)

    supers = LISTS * n_slots // SUPER + BUCKETS
    return pl.pallas_call(
        main_kernel,
        grid=(ION // 4,),
        out_shape=jax.ShapeDtypeStruct((ION, SL_DEV, PIX_DEV), F32),
        in_specs=[vmem] * 5
        + [
            pl.BlockSpec((4, 4 * HW, 2 * HW), lambda q: (q, 0, 0)),
            pl.BlockSpec((4, 8, 2 * HW), lambda q: (q, 0, 0)),
        ],
        out_specs=pl.BlockSpec((4, SL_DEV, PIX_DEV), lambda q: (q, 0, 0)),
        scratch_shapes=[
            pltpu.VMEM((groups, VAL, GROUP), BF),
            pltpu.VMEM((groups, GROUP), F32),
            pltpu.VMEM((groups, GROUP), F32),
            pltpu.VMEM((groups, GROUP), F32),
            pltpu.VMEM((8, n), I32),
            pltpu.VMEM((groups * PITCH, VAL), F32),
            pltpu.VMEM((supers * SUPER + STEP, VAL), F32),
            pltpu.VMEM((ION, BUCKETS * PX, SL_DEV), BF),
            pltpu.VMEM((ION * PX, SL_DEV), F32),
            pltpu.SMEM((8, n), I32),
            pltpu.SemaphoreType.DMA,
        ],
        compiler_params=pltpu.CompilerParams(vmem_limit_bytes=44 * 2**20),
        name="deposit_broaden",
    )(got, left, scan, first, tri, prof, norm)


def solution(mesh):
    in_specs = (
        P(None, ("los", "spec")),
        P(("los", "spec")),
        P(("los", "spec")),
        P(("los", "spec"), None),
        P(),
        P(),
        P(),
    )
    return jax.shard_map(
        on_device, mesh=mesh, in_specs=in_specs, out_specs=P(None, "los", "spec"), check_vma=False
    )
```

```python
import jax
import jax.numpy as jnp
from jax import lax
from jax.experimental import pallas as pl
from jax.experimental.pallas import tpu as pltpu
from jax.sharding import PartitionSpec as P

ELEM = 30
ION = 32
VAL = 32
WIDE = 3 * VAL
OUTS = ION + 16
BATCH = 4
HW = 64
SL_DEV = 256
PIX_DEV = 256
CAP = 32
DEAD = 256.0
NOWHERE = 512.0
LISTS = 3
GROUP = 256
SUPER = 256
PX = 16
SIDE = HW // PX
OWN = PIX_DEV // PX
BUCKETS = OWN + 2 * SIDE
QUAD = 8
STEP = 24
PITCH = GROUP + STEP
BF = jnp.bfloat16
F32 = jnp.float32
I32 = jnp.int32


def iota(shape, dim):
    return lax.broadcasted_iota(I32, shape, dim)


def nt(a, b):
    return lax.dot_general(a, b, (((1,), (1,)), ((), ())), preferred_element_type=F32)


def tn(a, b):
    return lax.dot_general(a, b, (((0,), (0,)), ((), ())), preferred_element_type=F32)


def swap_blocks(tiles):
    lane = iota((8, 128), 1)
    low = lane < 64
    even = (lane // 32) % 2 == 0
    far = [pltpu.roll(t, 64, 1) for t in tiles]
    half = [
        jnp.where(low, tiles[0], far[2]),
        jnp.where(low, tiles[1], far[3]),
        jnp.where(low, far[0], tiles[2]),
        jnp.where(low, far[1], tiles[3]),
    ]
    out = [None] * 4
    for p in (0, 2):
        a, b = half[p], half[p + 1]
        out[p] = jnp.where(even, a, pltpu.roll(b, 32, 1))
        out[p + 1] = jnp.where(even, pltpu.roll(a, 96, 1), b)
    return out


def pack_kernel(abund_hbm, line_hbm, pixel_hbm, counts_hbm, out_ref, abund_ref, line_ref, pixel_ref, counts_ref,
                sems, *, n_spec):
    copies = [
        pltpu.make_async_copy(src, dst, sems.at[k])
        for k, (src, dst) in enumerate(
            ((counts_hbm, counts_ref), (line_hbm, line_ref), (pixel_hbm, pixel_ref), (abund_hbm, abund_ref))
        )
    ]
    for copy in copies:
        copy.start()
    devices = counts_ref.shape[1]
    quads = devices // 4
    row = iota((quads, devices), 0)
    col = iota((quads, devices), 1)
    pick = jnp.where(iota((devices, 128), 0) % 4 == iota((devices, 128), 1) // CAP, 1.0, 0.0).astype(BF)
    slot = (iota((quads, 128), 1) % CAP).astype(F32)
    copies[0].wait()
    spread = jnp.where(col // 4 == row, counts_ref[...].astype(F32), 0.0).astype(BF)
    live_count = jnp.dot(spread, pick, preferred_element_type=F32)
    copies[1].wait()
    line = jnp.where(slot < live_count, line_ref[...].astype(F32), DEAD)
    copies[2].wait()
    pixel = pixel_ref[...].astype(F32)
    copies[3].wait()
    for t in range(devices // n_spec):
        msgs = []
        for a in range(t * n_spec // 4, (t + 1) * n_spec // 4):
            ab = abund_ref[:, a * 128 : (a + 1) * 128].astype(F32)
            vals = jnp.concatenate([ab, line[a : a + 1], pixel[a : a + 1]], axis=0)
            msgs += swap_blocks([vals[8 * j : 8 * j + 8] for j in range(4)])
        for b in range(0, n_spec, 2):
            parts = []
            for c in (b, b + 1):
                parts += [msgs[c], msgs[(c - 1) % n_spec], msgs[(c + 1) % n_spec]]
            out_ref[(t * n_spec + b) // 2] = jnp.concatenate(parts, axis=0).astype(BF)


def prepare_kernel(doppler_ref, share_ref, table_ref, prof_ref, norm_ref, left_ref, scan_ref, first_ref, tri_ref):
    offset = iota((4 * HW, 2 * HW), 1) + HW - iota((4 * HW, 2 * HW), 0)
    near = jnp.abs(offset) <= HW
    offset = offset.astype(F32)

    def body(i, carry):
        share = share_ref[i]
        u = offset / doppler_ref[i]
        raw = (1.0 - share) * jnp.exp(-u * u) + share / (1.0 + u * u)
        raw = jnp.where(near, raw, 0.0)
        prof_ref[i] = raw.astype(BF)
        norm_ref[i] = jnp.broadcast_to(1.0 / jnp.sum(raw, axis=0, keepdims=True), (8, 2 * HW))
        return carry

    lax.fori_loop(0, ION, body, 0)

    table = table_ref[...]
    hi = table.astype(BF)
    rest = table - hi.astype(F32)
    mid = rest.astype(BF)
    low = (rest - mid.astype(F32)).astype(BF)
    picks = jnp.where(iota((16, WIDE), 1) == iota((16, WIDE), 0) + ELEM, 1.0, 0.0)
    picks = jnp.where(iota((16, WIDE), 0) < 2, picks, 0.0).astype(BF)
    left_ref[...] = jnp.concatenate([jnp.concatenate([hi, mid, low], axis=1), picks], axis=0)

    n = scan_ref.shape[0]
    per = n // BUCKETS
    x, y = iota((n, n), 0), iota((n, n), 1)
    xb, yb = x // per, y // per
    kind = lambda b: jnp.where(b < SIDE, 1, jnp.where(b < SIDE + OWN, 0, 2))
    one = lambda m: jnp.where(m, 1.0, 0.0).astype(BF)
    scan_ref[:, :n] = one((xb == yb) & (x < y))
    scan_ref[:, n : 2 * n] = one((kind(xb) == kind(yb)) & (x % per == y % per) & (x < y))
    scan_ref[:, 2 * n :] = one(xb == yb)
    first_ref[...] = one((x % per == 0) & (xb < yb))
    tri_ref[...] = one(iota((GROUP, GROUP), 0) < iota((GROUP, GROUP), 1))


def unpack(recv_ref, rec_ref, line_ref, pixel_ref, per):
    def body(g, carry):
        tiles = []
        for p in range(4):
            block = recv_ref[g * 4 + p].astype(F32)
            tiles.append([block[8 * m : 8 * m + 8] for m in range(2 * LISTS)])
        for kind in range(LISTS):
            halves = []
            for h in range(2):
                srcs = [tiles[2 * h + s // 2][LISTS * (s % 2) + kind] for s in range(4)]
                halves.append(jnp.concatenate(swap_blocks(srcs), axis=0))
            rec = jnp.concatenate(halves, axis=1)
            rec_ref[kind * per + g] = jnp.concatenate([rec.astype(BF)] * 3, axis=0)
            line_ref[pl.ds(kind * per + g, 1), :] = rec[ELEM : ELEM + 1]
            pixel_ref[pl.ds(kind * per + g, 1), :] = rec[ELEM + 1 : ELEM + 2]
        return carry

    lax.fori_loop(0, per, body, 0, unroll=4)


def rank_slots(line_ref, pixel_ref, scan_ref, first_ref, tri_ref, pos_ref, info_ref, per):
    live = line_ref[...] < SL_DEV
    block = jnp.where(live, jnp.floor(pixel_ref[...] * (1.0 / PX)), -1.0)
    marks = []
    for b in range(BUCKETS):
        if b < SIDE:
            kind, which = 1, OWN - SIDE + b
        elif b < SIDE + OWN:
            kind, which = 0, b - SIDE
        else:
            kind, which = 2, b - SIDE - OWN
        marks.append(jnp.where(block[kind * per : (kind + 1) * per] == which, 1.0, 0.0).astype(BF))
    marks = jnp.concatenate(marks, axis=0)
    n = BUCKETS * per
    rank = jnp.dot(marks, tri_ref[...], preferred_element_type=F32)
    total = jnp.dot(marks, jnp.ones((GROUP, GROUP), BF), preferred_element_type=F32)
    count = nt(jnp.ones((8, GROUP), BF), marks)
    for kind, (lo, hi) in enumerate(((SIDE, SIDE + OWN), (0, SIDE), (SIDE + OWN, BUCKETS))):
        start = jnp.zeros((per, GROUP), F32)
        place = jnp.zeros((per, GROUP), F32)
        used = jnp.zeros((per, GROUP), F32)
        for b in range(lo, hi):
            rows = slice(b * per, (b + 1) * per)
            mark = marks[rows].astype(F32)
            place = place + mark * (start + rank[rows])
            used = used + mark
            start = start + total[rows]
        pos_ref[kind * per : (kind + 1) * per] = jnp.where(used > 0, place, NOWHERE)
    sums = jnp.dot(count.astype(BF), scan_ref[...], preferred_element_type=F32)
    ahead, source, whole = sums[:, :n], sums[:, n : 2 * n], sums[:, 2 * n :]
    supers = jnp.maximum(jnp.floor((whole + (SUPER - 1)) * (1.0 / SUPER)), 1.0)
    first = jnp.dot(supers.astype(BF), first_ref[...], preferred_element_type=F32)
    lane = iota((8, n), 1)
    b = lane // per
    kind = jnp.where(b < SIDE, 1, jnp.where(b < SIDE + OWN, 0, 2))
    base = ((kind * per + lane % per) * PITCH).astype(F32)
    longest = jnp.broadcast_to(jnp.max(count, axis=1, keepdims=True), (8, n))
    row = iota((8, n), 0)
    info = jnp.zeros((8, n), F32)
    for k, value in enumerate((source + base, first * SUPER + ahead, count, first, whole, supers, longest)):
        info = jnp.where(row == k, value, info)
    info_ref[...] = info.astype(I32)


def sort_groups(rec_ref, pos_ref, sorted_ref, groups):
    target = iota((GROUP, GROUP), 0).astype(F32).astype(BF)

    def body(g, carry):
        pos = jnp.broadcast_to(pos_ref[pl.ds(g, 1), :], (16, GROUP)).astype(BF)
        pos = jnp.concatenate([pos] * (GROUP // 16), axis=0)
        perm = jnp.where(pos == target, jnp.ones((), BF), jnp.zeros((), BF))
        sorted_ref[pl.ds(pl.multiple_of(g * PITCH, 8), GROUP), :] = nt(perm, rec_ref[g])
        return carry

    lax.fori_loop(0, groups, body, 0, unroll=16)


def join_runs(info, sorted_ref, rows_ref, n):
    def body(k, carry):
        rows_ref[pl.ds(info[1, k], STEP), :] = sorted_ref[pl.ds(info[0, k], STEP), :]
        return carry

    lax.fori_loop(0, n, body, 0, unroll=32)

    @pl.when(info[6, 0] > STEP)
    def _():
        def tail(k, carry):
            def one(r, c):
                rows_ref[pl.ds(info[1, k] + r, 1), :] = sorted_ref[pl.ds(info[0, k] + r, 1), :]
                return c

            lax.fori_loop(STEP, info[2, k], one, 0)
            return carry

        lax.fori_loop(0, n, tail, 0)


def make_columns(info, left_ref, rows_ref, cols_ref, per):
    def body(k, carry):
        at = pl.multiple_of(k * (BATCH * SUPER), BATCH * SUPER)
        got = nt(left_ref[...], rows_ref[pl.ds(at, BATCH * SUPER), :].astype(BF))
        for m in range(BATCH):
            cols_ref[k * BATCH + m] = got[:, m * SUPER : (m + 1) * SUPER]
        return carry

    lax.fori_loop(0, BUCKETS // BATCH, body, 0, unroll=6)
    last = (BUCKETS - 1) * per
    lax.fori_loop(BUCKETS // BATCH, (info[3, last] + info[5, last] + BATCH - 1) // BATCH, body, 0)


def deposit(info, cols_ref, grid_ref, acc_ref, per):
    lane = iota((1, SUPER), 1)
    pixels = iota((PX, SUPER), 0).astype(F32).astype(BF)
    lines = iota((SL_DEV, SUPER), 0).astype(F32).astype(BF)
    one, zero = jnp.ones((), BF), jnp.zeros((), BF)

    def packed(row):
        return jnp.broadcast_to(row, (16, SUPER)).astype(BF)

    def product(s, count):
        pixel = cols_ref[s, ION + 1 : ION + 2, :]
        pixel = jnp.where(lane < count, pixel - PX * jnp.floor(pixel * (1.0 / PX)), NOWHERE)
        here = packed(pixel) == pixels
        spread = [jnp.where(here, packed(cols_ref[s, i : i + 1, :]), zero) for i in range(ION)]
        line = jnp.concatenate([packed(cols_ref[s, ION : ION + 1, :])] * (SL_DEV // 16), axis=0)
        return nt(jnp.concatenate(spread, axis=0), jnp.where(line == lines, one, zero))

    def store(b, value):
        at = pl.ds(pl.multiple_of(b * PX, PX), PX)
        for i in range(ION):
            grid_ref[i, at, :] = value[i * PX : (i + 1) * PX].astype(BF)

    def body(b, carry):
        store(b, product(info[3, b * per], info[4, b * per]))
        return carry

    lax.fori_loop(0, BUCKETS, body, 0, unroll=12)

    last = (BUCKETS - 1) * per

    @pl.when(info[3, last] + info[5, last] > BUCKETS)
    def _():
        def again(b, carry):
            k = b * per

            @pl.when(info[5, k] > 1)
            def _():
                acc_ref[...] = jnp.zeros_like(acc_ref)

                def more(s, c):
                    acc_ref[...] += product(info[3, k] + s, info[4, k] - s * SUPER)
                    return c

                lax.fori_loop(0, info[5, k], more, 0)
                store(b, acc_ref[...])

            return carry

        lax.fori_loop(0, BUCKETS, again, 0)


def broaden(grid_ref, prof_ref, norm_ref, out_hbm, out_ref, sem):
    def copy(q):
        part = pl.ds(q * QUAD, QUAD)
        return pltpu.make_async_copy(out_ref.at[part], out_hbm.at[part], sem)

    def body(q, carry):
        for j in range(QUAD):
            i = q * QUAD + j
            plane = grid_ref[i]
            norm = norm_ref[i, 0:1]
            out_ref[i, :, :128] = tn(plane[:256], prof_ref[i]) * norm
            out_ref[i, :, 128:] = tn(plane[128:], prof_ref[i]) * norm
        copy(q).start()
        return carry

    lax.fori_loop(0, ION // QUAD, body, 0)
    pltpu.make_async_copy(out_ref, out_hbm, sem).wait()


def main_kernel(recv_ref, left_ref, scan_ref, first_ref, tri_ref, prof_ref, norm_ref, out_hbm, rec_ref, line_ref,
                pixel_ref, pos_ref, info_ref, sorted_ref, rows_ref, cols_ref, grid_ref, acc_ref, out_ref, info, sem,
                out_sem):
    groups = rec_ref.shape[0]
    per = groups // LISTS
    unpack(recv_ref, rec_ref, line_ref, pixel_ref, per)
    rank_slots(line_ref, pixel_ref, scan_ref, first_ref, tri_ref, pos_ref, info_ref, per)
    copy = pltpu.make_async_copy(info_ref, info, sem)
    copy.start()
    sort_groups(rec_ref, pos_ref, sorted_ref, groups)
    copy.wait()
    join_runs(info, sorted_ref, rows_ref, BUCKETS * per)
    make_columns(info, left_ref, rows_ref, cols_ref, per)
    deposit(info, cols_ref, grid_ref, acc_ref, per)
    broaden(grid_ref, prof_ref, norm_ref, out_hbm, out_ref, out_sem)


def on_device(abundances, sightline, pixel, counts, ion_table, doppler, lorentz_share):
    n_spec = lax.axis_size("spec")
    devices = lax.axis_size("los") * n_spec
    n_slots = abundances.shape[1]
    vmem = pl.BlockSpec(memory_space=pltpu.VMEM)
    smem = pl.BlockSpec(memory_space=pltpu.SMEM)
    anywhere = pl.BlockSpec(memory_space=pltpu.HBM)
    sent = pl.pallas_call(
        lambda *refs: pack_kernel(*refs, n_spec=n_spec),
        out_shape=jax.ShapeDtypeStruct((devices // 2, 2 * LISTS * 8, 128), BF),
        in_specs=[anywhere] * 4,
        out_specs=vmem,
        scratch_shapes=[
            pltpu.VMEM(abundances.shape, BF),
            pltpu.VMEM((n_slots // 128, 128), I32),
            pltpu.VMEM((n_slots // 128, 128), I32),
            pltpu.VMEM(counts.shape, I32),
            pltpu.SemaphoreType.DMA((4,)),
        ],
        compiler_params=pltpu.CompilerParams(vmem_limit_bytes=63 * 2**20),
        name="pack",
    )(abundances, sightline.reshape(n_slots // 128, 128), pixel.reshape(n_slots // 128, 128), counts)
    groups = LISTS * n_slots // GROUP
    n = BUCKETS * groups // LISTS
    table = jnp.pad(ion_table.T, ((0, 0), (0, VAL - ELEM)))
    prof, norm, left, scan, first, tri = pl.pallas_call(
        prepare_kernel,
        out_shape=[
            jax.ShapeDtypeStruct((ION, 4 * HW, 2 * HW), BF),
            jax.ShapeDtypeStruct((ION, 8, 2 * HW), F32),
            jax.ShapeDtypeStruct((OUTS, WIDE), BF),
            jax.ShapeDtypeStruct((n, 3 * n), BF),
            jax.ShapeDtypeStruct((n, n), BF),
            jax.ShapeDtypeStruct((GROUP, GROUP), BF),
        ],
        in_specs=[smem, smem, vmem],
        out_specs=[vmem] * 6,
        compiler_params=pltpu.CompilerParams(vmem_limit_bytes=10 * 2**20),
        cost_estimate=pl.CostEstimate(flops=20_000_000, bytes_accessed=4 * 2**20, transcendentals=3_000_000),
        name="prepare",
    )(doppler, lorentz_share, table)
    got = lax.all_to_all(
        sent.reshape(devices, LISTS * 8, 128), ("los", "spec"), split_axis=0, concat_axis=0, tiled=True
    ).reshape(devices // 2, 2 * LISTS * 8, 128)

    supers = LISTS * n_slots // SUPER + BUCKETS
    return pl.pallas_call(
        main_kernel,
        out_shape=jax.ShapeDtypeStruct((ION, SL_DEV, PIX_DEV), F32),
        in_specs=[vmem] * 7,
        out_specs=anywhere,
        scratch_shapes=[
            pltpu.VMEM((groups, WIDE, GROUP), BF),
            pltpu.VMEM((groups, GROUP), F32),
            pltpu.VMEM((groups, GROUP), F32),
            pltpu.VMEM((groups, GROUP), F32),
            pltpu.VMEM((8, n), I32),
            pltpu.VMEM((groups * PITCH, WIDE), F32),
            pltpu.VMEM((supers * SUPER + STEP, WIDE), F32),
            pltpu.VMEM((supers, OUTS, SUPER), F32),
            pltpu.VMEM((ION, BUCKETS * PX, SL_DEV), BF),
            pltpu.VMEM((ION * PX, SL_DEV), F32),
            pltpu.VMEM((ION, SL_DEV, PIX_DEV), F32),
            pltpu.SMEM((8, n), I32),
            pltpu.SemaphoreType.DMA,
            pltpu.SemaphoreType.DMA,
        ],
        compiler_params=pltpu.CompilerParams(vmem_limit_bytes=46 * 2**20),
        name="deposit_broaden",
    )(got, left, scan, first, tri, prof, norm)


def solution(mesh):
    in_specs = (
        P(None, ("los", "spec")),
        P(("los", "spec")),
        P(("los", "spec")),
        P(("los", "spec"), None),
        P(),
        P(),
        P(),
    )
    return jax.shard_map(
        on_device, mesh=mesh, in_specs=in_specs, out_specs=P(None, "los", "spec"), check_vma=False
    )
```

```python
import jax
import jax.numpy as jnp
from jax import lax
from jax.experimental import pallas as pl
from jax.experimental.pallas import tpu as pltpu
from jax.sharding import PartitionSpec as P

ELEM = 30
ION = 32
VAL = 32
WIDE = 3 * VAL
OUTS = ION + 16
BATCH = 4
HW = 64
SL_DEV = 256
PIX_DEV = 256
CAP = 32
DEAD = 256.0
NOWHERE = 512.0
LISTS = 3
GROUP = 256
SUPER = 256
PX = 16
SIDE = HW // PX
OWN = PIX_DEV // PX
BUCKETS = OWN + 2 * SIDE
QUAD = 8
STEP = 24
PITCH = GROUP + STEP
BF = jnp.bfloat16
F32 = jnp.float32
I32 = jnp.int32


def iota(shape, dim):
    return lax.broadcasted_iota(I32, shape, dim)


def nt(a, b):
    return lax.dot_general(a, b, (((1,), (1,)), ((), ())), preferred_element_type=F32)


def tn(a, b):
    return lax.dot_general(a, b, (((0,), (0,)), ((), ())), preferred_element_type=F32)


def swap_blocks(tiles):
    lane = iota((8, 128), 1)
    low = lane < 64
    even = (lane // 32) % 2 == 0
    far = [pltpu.roll(t, 64, 1) for t in tiles]
    half = [
        jnp.where(low, tiles[0], far[2]),
        jnp.where(low, tiles[1], far[3]),
        jnp.where(low, far[0], tiles[2]),
        jnp.where(low, far[1], tiles[3]),
    ]
    out = [None] * 4
    for p in (0, 2):
        a, b = half[p], half[p + 1]
        out[p] = jnp.where(even, a, pltpu.roll(b, 32, 1))
        out[p + 1] = jnp.where(even, pltpu.roll(a, 96, 1), b)
    return out


def pack_kernel(abund_hbm, line_hbm, pixel_hbm, counts_hbm, out_ref, abund_ref, line_ref, pixel_ref, counts_ref,
                sems, *, n_spec):
    copies = [
        pltpu.make_async_copy(src, dst, sems.at[k])
        for k, (src, dst) in enumerate(
            ((counts_hbm, counts_ref), (line_hbm, line_ref), (pixel_hbm, pixel_ref), (abund_hbm, abund_ref))
        )
    ]
    for copy in copies:
        copy.start()
    devices = counts_ref.shape[1]
    quads = devices // 4
    row = iota((quads, devices), 0)
    col = iota((quads, devices), 1)
    pick = jnp.where(iota((devices, 128), 0) % 4 == iota((devices, 128), 1) // CAP, 1.0, 0.0).astype(BF)
    slot = (iota((quads, 128), 1) % CAP).astype(F32)
    copies[0].wait()
    spread = jnp.where(col // 4 == row, counts_ref[...].astype(F32), 0.0).astype(BF)
    live_count = jnp.dot(spread, pick, preferred_element_type=F32)
    copies[1].wait()
    line = jnp.where(slot < live_count, line_ref[...].astype(F32), DEAD)
    copies[2].wait()
    pixel = pixel_ref[...].astype(F32)
    copies[3].wait()
    for t in range(devices // n_spec):
        msgs = []
        for a in range(t * n_spec // 4, (t + 1) * n_spec // 4):
            ab = abund_ref[:, a * 128 : (a + 1) * 128].astype(F32)
            vals = jnp.concatenate([ab, line[a : a + 1], pixel[a : a + 1]], axis=0)
            msgs += swap_blocks([vals[8 * j : 8 * j + 8] for j in range(4)])
        for b in range(0, n_spec, 2):
            parts = []
            for c in (b, b + 1):
                parts += [msgs[c], msgs[(c - 1) % n_spec], msgs[(c + 1) % n_spec]]
            out_ref[(t * n_spec + b) // 2] = jnp.concatenate(parts, axis=0).astype(BF)


def prepare_kernel(doppler_ref, share_ref, table_ref, prof_ref, norm_ref, left_ref, scan_ref, tri_ref):
    offset = iota((4 * HW, 2 * HW), 1) + HW - iota((4 * HW, 2 * HW), 0)
    near = jnp.abs(offset) <= HW
    offset = offset.astype(F32)

    def body(i, carry):
        share = share_ref[i]
        u = offset / doppler_ref[i]
        raw = (1.0 - share) * jnp.exp(-u * u) + share / (1.0 + u * u)
        raw = jnp.where(near, raw, 0.0)
        prof_ref[i] = raw.astype(BF)
        norm_ref[i] = jnp.broadcast_to(1.0 / jnp.sum(raw, axis=0, keepdims=True), (8, 2 * HW))
        return carry

    lax.fori_loop(0, ION, body, 0)

    table = table_ref[...]
    hi = table.astype(BF)
    rest = table - hi.astype(F32)
    mid = rest.astype(BF)
    low = (rest - mid.astype(F32)).astype(BF)
    picks = jnp.where(iota((16, WIDE), 1) == iota((16, WIDE), 0) + ELEM, 1.0, 0.0)
    picks = jnp.where(iota((16, WIDE), 0) < 2, picks, 0.0).astype(BF)
    left_ref[...] = jnp.concatenate([jnp.concatenate([hi, mid, low], axis=1), picks], axis=0)

    x, y = iota((128, 128), 0), iota((128, 128), 1)
    one = lambda m: jnp.where(m, 1.0, 0.0).astype(BF)
    bucket, group, half = x // 16 == y // 16, x % 16 == y % 16, x // 64 == y // 64
    for k, m in enumerate(
        (
            bucket & (x < y),
            bucket,
            group & half & (x < y),
            group & (x < y),
            group & (x >= 64),
            group & (y < 64),
            group & (x >= 64) & (y < 64),
            (x % 16 == 0) & (x // 16 < y // 16),
            x % 16 == 0,
        )
    ):
        scan_ref[k] = one(m)
    tri_ref[...] = one(iota((GROUP, GROUP), 0) < iota((GROUP, GROUP), 1))


def unpack(recv_ref, rec_ref, line_ref, pixel_ref, per):
    def body(g, carry):
        tiles = []
        for p in range(4):
            block = recv_ref[g * 4 + p].astype(F32)
            tiles.append([block[8 * m : 8 * m + 8] for m in range(2 * LISTS)])
        for kind in range(LISTS):
            halves = []
            for h in range(2):
                srcs = [tiles[2 * h + s // 2][LISTS * (s % 2) + kind] for s in range(4)]
                halves.append(jnp.concatenate(swap_blocks(srcs), axis=0))
            rec = jnp.concatenate(halves, axis=1)
            rec_ref[kind * per + g] = jnp.concatenate([rec.astype(BF)] * 3, axis=0)
            line_ref[pl.ds(kind * per + g, 1), :] = rec[ELEM : ELEM + 1]
            pixel_ref[pl.ds(kind * per + g, 1), :] = rec[ELEM + 1 : ELEM + 2]
        return carry

    lax.fori_loop(0, per, body, 0, unroll=4)


def rank_slots(line_ref, pixel_ref, scan_ref, tri_ref, pos_ref, info_ref, per):
    live = line_ref[...] < SL_DEV
    block = jnp.where(live, jnp.floor(pixel_ref[...] * (1.0 / PX)), -1.0)
    marks = []
    for b in range(BUCKETS):
        if b < SIDE:
            kind, which = 1, OWN - SIDE + b
        elif b < SIDE + OWN:
            kind, which = 0, b - SIDE
        else:
            kind, which = 2, b - SIDE - OWN
        marks.append(jnp.where(block[kind * per : (kind + 1) * per] == which, 1.0, 0.0).astype(BF))
    marks = jnp.concatenate(marks, axis=0)
    n = BUCKETS * per
    rank = jnp.dot(marks, tri_ref[...], preferred_element_type=F32)
    total = jnp.dot(marks, jnp.ones((GROUP, GROUP), BF), preferred_element_type=F32)
    count = nt(jnp.ones((8, GROUP), BF), marks)
    for kind, (lo, hi) in enumerate(((SIDE, SIDE + OWN), (0, SIDE), (SIDE + OWN, BUCKETS))):
        start = jnp.zeros((per, GROUP), F32)
        place = jnp.zeros((per, GROUP), F32)
        used = jnp.zeros((per, GROUP), F32)
        for b in range(lo, hi):
            rows = slice(b * per, (b + 1) * per)
            mark = marks[rows].astype(F32)
            place = place + mark * (start + rank[rows])
            used = used + mark
            start = start + total[rows]
        pos_ref[kind * per : (kind + 1) * per] = jnp.where(used > 0, place, NOWHERE)
    times = lambda a, k: jnp.dot(a, scan_ref[k], preferred_element_type=F32)
    join = lambda a: jnp.concatenate(a, axis=1)
    c = [count[:, 128 * k : 128 * k + 128].astype(BF) for k in range(3)]
    ahead, whole = (join([times(a, k) for a in c]) for k in (0, 1))
    source = join(
        [
            times(c[0], 2),
            times(c[1], 3) + times(c[0], 4),
            times(c[2], 2) + times(c[1], 5) + times(c[0], 6),
        ]
    )
    supers = jnp.maximum(jnp.floor((whole + (SUPER - 1)) * (1.0 / SUPER)), 1.0)
    d = [supers[:, 128 * k : 128 * k + 128].astype(BF) for k in range(3)]
    first = join(
        [
            times(d[0], 7),
            times(d[1], 7) + times(d[0], 8),
            times(d[2], 7) + times(d[1], 8) + times(d[0], 8),
        ]
    )
    lane = iota((8, n), 1)
    b = lane // per
    kind = jnp.where(b < SIDE, 1, jnp.where(b < SIDE + OWN, 0, 2))
    base = ((kind * per + lane % per) * PITCH).astype(F32)
    longest = jnp.broadcast_to(jnp.max(count, axis=1, keepdims=True), (8, n))
    row = iota((8, n), 0)
    info = jnp.zeros((8, n), F32)
    for k, value in enumerate((source + base, first * SUPER + ahead, count, first, whole, supers, longest)):
        info = jnp.where(row == k, value, info)
    info_ref[...] = info.astype(I32)


def sort_groups(rec_ref, pos_ref, sorted_ref, groups):
    target = iota((GROUP, GROUP), 0).astype(F32).astype(BF)

    def body(g, carry):
        pos = jnp.broadcast_to(pos_ref[pl.ds(g, 1), :], (16, GROUP)).astype(BF)
        pos = jnp.concatenate([pos] * (GROUP // 16), axis=0)
        perm = jnp.where(pos == target, jnp.ones((), BF), jnp.zeros((), BF))
        sorted_ref[pl.ds(pl.multiple_of(g * PITCH, 8), GROUP), :] = nt(perm, rec_ref[g])
        return carry

    lax.fori_loop(0, groups, body, 0, unroll=16)


def join_runs(info, sorted_ref, rows_ref, n):
    def body(k, carry):
        rows_ref[pl.ds(info[1, k], STEP), :] = sorted_ref[pl.ds(info[0, k], STEP), :]
        return carry

    lax.fori_loop(0, n, body, 0, unroll=32)

    @pl.when(info[6, 0] > STEP)
    def _():
        def tail(k, carry):
            def one(r, c):
                rows_ref[pl.ds(info[1, k] + r, 1), :] = sorted_ref[pl.ds(info[0, k] + r, 1), :]
                return c

            lax.fori_loop(STEP, info[2, k], one, 0)
            return carry

        lax.fori_loop(0, n, tail, 0)


def make_columns(info, left_ref, rows_ref, cols_ref, per):
    def body(k, carry):
        at = pl.multiple_of(k * (BATCH * SUPER), BATCH * SUPER)
        got = nt(left_ref[...], rows_ref[pl.ds(at, BATCH * SUPER), :].astype(BF))
        for m in range(BATCH):
            cols_ref[k * BATCH + m] = got[:, m * SUPER : (m + 1) * SUPER]
        return carry

    lax.fori_loop(0, BUCKETS // BATCH, body, 0, unroll=6)
    last = (BUCKETS - 1) * per
    lax.fori_loop(BUCKETS // BATCH, (info[3, last] + info[5, last] + BATCH - 1) // BATCH, body, 0)


def deposit(info, cols_ref, grid_ref, acc_ref, per):
    lane = iota((1, SUPER), 1)
    pixels = iota((PX, SUPER), 0).astype(F32).astype(BF)
    lines = iota((SL_DEV, SUPER), 0).astype(F32).astype(BF)
    one, zero = jnp.ones((), BF), jnp.zeros((), BF)

    def packed(row):
        return jnp.broadcast_to(row, (16, SUPER)).astype(BF)

    def product(s, count):
        pixel = cols_ref[s, ION + 1 : ION + 2, :]
        pixel = jnp.where(lane < count, pixel - PX * jnp.floor(pixel * (1.0 / PX)), NOWHERE)
        here = packed(pixel) == pixels
        spread = [jnp.where(here, packed(cols_ref[s, i : i + 1, :]), zero) for i in range(ION)]
        line = jnp.concatenate([packed(cols_ref[s, ION : ION + 1, :])] * (SL_DEV // 16), axis=0)
        return nt(jnp.concatenate(spread, axis=0), jnp.where(line == lines, one, zero))

    def store(b, value):
        at = pl.ds(pl.multiple_of(b * PX, PX), PX)
        for i in range(ION):
            grid_ref[i, at, :] = value[i * PX : (i + 1) * PX].astype(BF)

    def body(b, carry):
        store(b, product(info[3, b * per], info[4, b * per]))
        return carry

    lax.fori_loop(0, BUCKETS, body, 0, unroll=12)

    last = (BUCKETS - 1) * per

    @pl.when(info[3, last] + info[5, last] > BUCKETS)
    def _():
        def again(b, carry):
            k = b * per

            @pl.when(info[5, k] > 1)
            def _():
                acc_ref[...] = jnp.zeros_like(acc_ref)

                def more(s, c):
                    acc_ref[...] += product(info[3, k] + s, info[4, k] - s * SUPER)
                    return c

                lax.fori_loop(0, info[5, k], more, 0)
                store(b, acc_ref[...])

            return carry

        lax.fori_loop(0, BUCKETS, again, 0)


def broaden(grid_ref, prof_ref, norm_ref, out_hbm, out_ref, sem):
    def body(q, carry):
        for j in range(QUAD):
            i = q * QUAD + j
            plane = grid_ref[i]
            norm = norm_ref[i, 0:1]
            out_ref[i, :, :128] = tn(plane[:256], prof_ref[i]) * norm
            out_ref[i, :, 128:] = tn(plane[128:], prof_ref[i]) * norm
            pltpu.make_async_copy(out_ref.at[i], out_hbm.at[i], sem).start()
        return carry

    lax.fori_loop(0, ION // QUAD, body, 0)
    pltpu.make_async_copy(out_ref, out_hbm, sem).wait()


def main_kernel(recv_ref, left_ref, norm_ref, scan_ref, tri_ref, prof_ref, out_hbm, rec_ref, line_ref, pixel_ref,
                pos_ref, info_ref, sorted_ref, rows_ref, cols_ref, grid_ref, acc_ref, out_ref, info, sem, out_sem):
    groups = rec_ref.shape[0]
    per = groups // LISTS
    unpack(recv_ref, rec_ref, line_ref, pixel_ref, per)
    rank_slots(line_ref, pixel_ref, scan_ref, tri_ref, pos_ref, info_ref, per)
    to_scalars = pltpu.make_async_copy(info_ref, info, sem)
    to_scalars.start()
    sort_groups(rec_ref, pos_ref, sorted_ref, groups)
    to_scalars.wait()
    join_runs(info, sorted_ref, rows_ref, BUCKETS * per)
    make_columns(info, left_ref, rows_ref, cols_ref, per)
    deposit(info, cols_ref, grid_ref, acc_ref, per)
    broaden(grid_ref, prof_ref, norm_ref, out_hbm, out_ref, out_sem)


def on_device(abundances, sightline, pixel, counts, ion_table, doppler, lorentz_share):
    n_spec = lax.axis_size("spec")
    devices = lax.axis_size("los") * n_spec
    n_slots = abundances.shape[1]
    vmem = pl.BlockSpec(memory_space=pltpu.VMEM)
    smem = pl.BlockSpec(memory_space=pltpu.SMEM)
    anywhere = pl.BlockSpec(memory_space=pltpu.HBM)
    sent = pl.pallas_call(
        lambda *refs: pack_kernel(*refs, n_spec=n_spec),
        out_shape=jax.ShapeDtypeStruct((devices // 2, 2 * LISTS * 8, 128), BF),
        in_specs=[anywhere] * 4,
        out_specs=vmem,
        scratch_shapes=[
            pltpu.VMEM(abundances.shape, BF),
            pltpu.VMEM((n_slots // 128, 128), I32),
            pltpu.VMEM((n_slots // 128, 128), I32),
            pltpu.VMEM(counts.shape, I32),
            pltpu.SemaphoreType.DMA((4,)),
        ],
        compiler_params=pltpu.CompilerParams(vmem_limit_bytes=63 * 2**20),
        name="pack",
    )(abundances, sightline.reshape(n_slots // 128, 128), pixel.reshape(n_slots // 128, 128), counts)
    groups = LISTS * n_slots // GROUP
    n = BUCKETS * groups // LISTS
    table = jnp.pad(ion_table.T, ((0, 0), (0, VAL - ELEM)))
    prof, norm, left, scan, tri = pl.pallas_call(
        prepare_kernel,
        out_shape=[
            jax.ShapeDtypeStruct((ION, 4 * HW, 2 * HW), BF),
            jax.ShapeDtypeStruct((ION, 8, 2 * HW), F32),
            jax.ShapeDtypeStruct((OUTS, WIDE), BF),
            jax.ShapeDtypeStruct((9, 128, 128), BF),
            jax.ShapeDtypeStruct((GROUP, GROUP), BF),
        ],
        in_specs=[smem, smem, vmem],
        out_specs=[vmem] * 5,
        compiler_params=pltpu.CompilerParams(vmem_limit_bytes=10 * 2**20),
        cost_estimate=pl.CostEstimate(flops=20_000_000, bytes_accessed=4 * 2**20, transcendentals=3_000_000),
        name="prepare",
    )(doppler, lorentz_share, table)
    got = lax.all_to_all(
        sent.reshape(devices, LISTS * 8, 128), ("los", "spec"), split_axis=0, concat_axis=0, tiled=True
    ).reshape(devices // 2, 2 * LISTS * 8, 128)

    supers = LISTS * n_slots // SUPER + BUCKETS
    return pl.pallas_call(
        main_kernel,
        out_shape=jax.ShapeDtypeStruct((ION, SL_DEV, PIX_DEV), F32),
        in_specs=[vmem] * 6,
        out_specs=anywhere,
        scratch_shapes=[
            pltpu.VMEM((groups, WIDE, GROUP), BF),
            pltpu.VMEM((groups, GROUP), F32),
            pltpu.VMEM((groups, GROUP), F32),
            pltpu.VMEM((groups, GROUP), F32),
            pltpu.VMEM((8, n), I32),
            pltpu.VMEM((groups * PITCH, WIDE), F32),
            pltpu.VMEM((supers * SUPER + STEP, WIDE), F32),
            pltpu.VMEM((supers, OUTS, SUPER), F32),
            pltpu.VMEM((ION, BUCKETS * PX, SL_DEV), BF),
            pltpu.VMEM((ION * PX, SL_DEV), F32),
            pltpu.VMEM((ION, SL_DEV, PIX_DEV), F32),
            pltpu.SMEM((8, n), I32),
            pltpu.SemaphoreType.DMA,
            pltpu.SemaphoreType.DMA,
        ],
        compiler_params=pltpu.CompilerParams(vmem_limit_bytes=46 * 2**20),
        name="deposit_broaden",
    )(got, left, norm, scan, tri, prof)


def solution(mesh):
    in_specs = (
        P(None, ("los", "spec")),
        P(("los", "spec")),
        P(("los", "spec")),
        P(("los", "spec"), None),
        P(),
        P(),
        P(),
    )
    return jax.shard_map(
        on_device, mesh=mesh, in_specs=in_specs, out_specs=P(None, "los", "spec"), check_vma=False
    )
```

```python
import jax
import jax.numpy as jnp
from jax import lax
from jax.experimental import pallas as pl
from jax.experimental.pallas import tpu as pltpu
from jax.sharding import PartitionSpec as P

ELEM = 30
ION = 32
VAL = 32
WIDE = 3 * VAL
OUTS = ION + 16
BATCH = 4
HW = 64
SL_DEV = 256
PIX_DEV = 256
PIXELS = 4096
CAP = 32
DEAD = 256.0
MARK = 384.0
NOWHERE = 512.0
LISTS = 2
GROUP = 256
SUPER = 256
PX = 16
SIDE = HW // PX
OWN = PIX_DEV // PX
BUCKETS = OWN + 2 * SIDE
QUAD = 16
STEP = 24
PITCH = GROUP + STEP
SENT_TILES = 2
BF = jnp.bfloat16
F32 = jnp.float32
I32 = jnp.int32


def iota(shape, dim):
    return lax.broadcasted_iota(I32, shape, dim)


def nt(a, b):
    return lax.dot_general(a, b, (((1,), (1,)), ((), ())), preferred_element_type=F32)


def tn(a, b):
    return lax.dot_general(a, b, (((0,), (0,)), ((), ())), preferred_element_type=F32)


def swap_blocks(tiles):
    lane = iota((8, 128), 1)
    low = lane < 64
    even = (lane // 32) % 2 == 0
    far = [pltpu.roll(t, 64, 1) for t in tiles]
    half = [
        jnp.where(low, tiles[0], far[2]),
        jnp.where(low, tiles[1], far[3]),
        jnp.where(low, far[0], tiles[2]),
        jnp.where(low, far[1], tiles[3]),
    ]
    out = [None] * 4
    for p in (0, 2):
        a, b = half[p], half[p + 1]
        out[p] = jnp.where(even, a, pltpu.roll(b, 32, 1))
        out[p + 1] = jnp.where(even, pltpu.roll(a, 96, 1), b)
    return out


def pack_kernel(abund_hbm, line_hbm, pixel_hbm, counts_hbm, out_hbm, abund_ref, line_ref, pixel_ref, counts_ref,
                out_ref, sems, out_sem, *, n_spec):
    copies = [
        pltpu.make_async_copy(src, dst, sems.at[k])
        for k, (src, dst) in enumerate(
            ((counts_hbm, counts_ref), (line_hbm, line_ref), (pixel_hbm, pixel_ref), (abund_hbm, abund_ref))
        )
    ]
    for copy in copies:
        copy.start()
    devices = counts_ref.shape[1]
    quads = devices // 4
    per_tile = n_spec // 4
    one = lambda m: jnp.where(m, 1.0, 0.0).astype(BF)
    dot = lambda a, b: jnp.dot(a, b, preferred_element_type=F32)
    x, y = iota((128, 128), 0), iota((128, 128), 1)
    same = x // CAP == y // CAP
    lane = iota((quads, 128), 1)
    row = iota((quads, 128), 0)
    slot = (lane % CAP).astype(F32)
    pick = one(iota((devices, 128), 0) % 4 == iota((devices, 128), 1) // CAP)
    for copy in copies[:3]:
        copy.wait()
    owner = iota((quads, devices), 1) // 4 == iota((quads, devices), 0)
    live = slot < dot(jnp.where(owner, counts_ref[...].astype(F32), 0.0).astype(BF), pick)
    line = jnp.where(live, line_ref[...].astype(F32), DEAD)
    pixel = pixel_ref[...].astype(F32)

    low = jnp.where(live & (pixel < HW), 1.0, 0.0)
    high = jnp.where(live & (pixel >= PIX_DEV - HW), 1.0, 0.0)
    marks = jnp.concatenate([low, 1.0 - low - high, high], axis=0).astype(BF)
    rank = dot(marks, one(same & (x < y)))
    total = dot(marks, one(same))
    n_low, n_high = total[:quads], total[2 * quads :]
    place = jnp.where(high > 0, CAP - n_high + rank[2 * quads :], n_low + rank[quads : 2 * quads])
    place = jnp.where(low > 0, rank[:quads], place) + (lane // CAP * CAP).astype(F32)
    ends = jnp.concatenate([n_low, n_high], axis=0).astype(BF)
    ends = [dot(ends, one(x == CAP * b)) for b in range(4)]
    lows = [e[:quads] for e in ends]
    highs = [e[quads:] for e in ends]

    def turn(v, ahead):
        near, far = (quads - 1, per_tile - 1) if ahead else (1, quads - per_tile + 1)
        edge = row % per_tile == (per_tile - 1 if ahead else 0)
        return jnp.where(edge, pltpu.roll(v, far, 0), pltpu.roll(v, near, 0))

    used = [lows[1] + turn(highs[3], False), lows[2] + highs[0], lows[3] + highs[1], turn(lows[0], True) + highs[2]]
    used = jnp.maximum(jnp.maximum(used[0], used[1]), jnp.maximum(used[2], used[3]))
    line = jnp.where(jnp.max(used, axis=0, keepdims=True) > CAP, MARK, line)

    target = x.astype(F32).astype(BF)
    spot = (iota((8, 128), 1) % CAP).astype(F32)
    hole = (iota((8, 128), 0) == ELEM % 8) & (iota((8, 128), 1) // CAP == ELEM // 8)
    hole = jnp.where(hole, DEAD, 0.0)
    copies[3].wait()
    for t in range(devices // n_spec):
        msgs = []
        for a in range(t * per_tile, (t + 1) * per_tile):
            ab = abund_ref[:, a * 128 : (a + 1) * 128].astype(F32)
            vals = jnp.concatenate([ab, line[a : a + 1], pixel[a : a + 1]], axis=0).astype(BF)
            dest = jnp.broadcast_to(place[a : a + 1], (16, 128)).astype(BF)
            dest = jnp.concatenate([dest] * 8, axis=0)
            moved = nt(vals, jnp.where(dest == target, jnp.ones((), BF), jnp.zeros((), BF)))
            msgs += swap_blocks([moved[8 * j : 8 * j + 8] for j in range(4)])
        for c in range(n_spec):
            prev, after = (c - 1) % n_spec, (c + 1) % n_spec
            run = lambda v, k: v[k % 4][t * per_tile + k // 4 : t * per_tile + k // 4 + 1]
            halo = jnp.where(spot >= CAP - run(highs, prev), msgs[prev], hole)
            halo = jnp.where(spot < run(lows, after), msgs[after], halo)
            out_ref[t * n_spec + c] = jnp.concatenate([msgs[c], halo], axis=0).astype(BF)
        if (t + 1) % SENT_TILES == 0:
            part = pl.ds((t + 1 - SENT_TILES) * n_spec, SENT_TILES * n_spec)
            pltpu.make_async_copy(out_ref.at[part], out_hbm.at[part], out_sem).start()
    pltpu.make_async_copy(out_ref, out_hbm, out_sem).wait()


def prepare_kernel(doppler_ref, share_ref, table_ref, prof_ref, norm_ref, left_ref, scan_ref, tri_ref):
    offset = iota((4 * HW, 2 * HW), 1) + HW - iota((4 * HW, 2 * HW), 0)
    near = jnp.abs(offset) <= HW
    offset = offset.astype(F32)

    def body(i, carry):
        share = share_ref[i]
        u = offset / doppler_ref[i]
        raw = (1.0 - share) * jnp.exp(-u * u) + share / (1.0 + u * u)
        raw = jnp.where(near, raw, 0.0)
        prof_ref[i] = raw.astype(BF)
        norm_ref[i] = jnp.broadcast_to(1.0 / jnp.sum(raw, axis=0, keepdims=True), (8, 2 * HW))
        return carry

    lax.fori_loop(0, ION, body, 0)

    table = table_ref[...]
    hi = table.astype(BF)
    rest = table - hi.astype(F32)
    mid = rest.astype(BF)
    low = (rest - mid.astype(F32)).astype(BF)
    picks = jnp.where(iota((16, WIDE), 1) == iota((16, WIDE), 0) + ELEM, 1.0, 0.0)
    picks = jnp.where(iota((16, WIDE), 0) < 2, picks, 0.0).astype(BF)
    left_ref[...] = jnp.concatenate([jnp.concatenate([hi, mid, low], axis=1), picks], axis=0)

    x, y = iota((128, 128), 0), iota((128, 128), 1)
    one = lambda m: jnp.where(m, 1.0, 0.0).astype(BF)
    bucket, group, half = x // 16 == y // 16, x % 16 == y % 16, x // 64 == y // 64
    for k, m in enumerate(
        (
            bucket & (x < y),
            bucket,
            group & half & (x < y),
            group & (x < y),
            group & (x >= 64),
            group & (y < 64),
            group & (x // 64 != y // 64),
            (x % 16 == 0) & (x // 16 < y // 16),
            x % 16 == 0,
        )
    ):
        scan_ref[k] = one(m)
    tri_ref[...] = one(iota((GROUP, GROUP), 0) < iota((GROUP, GROUP), 1))


def unpack(recv_ref, rec_ref, line_ref, pixel_ref, per):
    def body(g, carry):
        tiles = [recv_ref[g * 8 + p].astype(F32) for p in range(8)]
        for kind in range(LISTS):
            halves = []
            for h in range(2):
                srcs = [tiles[4 * h + s][8 * kind : 8 * kind + 8] for s in range(4)]
                halves.append(jnp.concatenate(swap_blocks(srcs), axis=0))
            rec = jnp.concatenate(halves, axis=1)
            rec_ref[kind * per + g] = jnp.concatenate([rec.astype(BF)] * 3, axis=0)
            line_ref[pl.ds(kind * per + g, 1), :] = rec[ELEM : ELEM + 1]
            pixel_ref[pl.ds(kind * per + g, 1), :] = rec[ELEM + 1 : ELEM + 2]
        return carry

    lax.fori_loop(0, per, body, 0, unroll=4)


def rank_slots(line_ref, pixel_ref, scan_ref, tri_ref, pos_ref, info_ref, per):
    live = line_ref[...] < SL_DEV
    block = jnp.where(live, jnp.floor(pixel_ref[...] * (1.0 / PX)), -1.0)
    marks = []
    for b in range(BUCKETS):
        if b < SIDE:
            kind, which = 1, OWN - SIDE + b
        elif b < SIDE + OWN:
            kind, which = 0, b - SIDE
        else:
            kind, which = 1, b - SIDE - OWN
        marks.append(jnp.where(block[kind * per : (kind + 1) * per] == which, 1.0, 0.0).astype(BF))
    marks = jnp.concatenate(marks, axis=0)
    n = BUCKETS * per
    rank = jnp.dot(marks, tri_ref[...], preferred_element_type=F32)
    total = jnp.dot(marks, jnp.ones((GROUP, GROUP), BF), preferred_element_type=F32)
    count = nt(jnp.ones((8, GROUP), BF), marks)
    sides = [*range(SIDE), *range(SIDE + OWN, BUCKETS)]
    for kind, buckets in enumerate((range(SIDE, SIDE + OWN), sides)):
        start = jnp.zeros((per, GROUP), F32)
        place = jnp.zeros((per, GROUP), F32)
        used = jnp.zeros((per, GROUP), F32)
        for b in buckets:
            rows = slice(b * per, (b + 1) * per)
            mark = marks[rows].astype(F32)
            place = place + mark * (start + rank[rows])
            used = used + mark
            start = start + total[rows]
        pos_ref[kind * per : (kind + 1) * per] = jnp.where(used > 0, place, NOWHERE)
    times = lambda a, k: jnp.dot(a, scan_ref[k], preferred_element_type=F32)
    join = lambda a: jnp.concatenate(a, axis=1)
    c = [count[:, 128 * k : 128 * k + 128].astype(BF) for k in range(3)]
    ahead, whole = (join([times(a, k) for a in c]) for k in (0, 1))
    source = join(
        [
            times(c[0], 2),
            times(c[1], 3) + times(c[0], 4),
            times(c[2], 2) + times(c[1], 5) + times(c[0], 6),
        ]
    )
    supers = jnp.maximum(jnp.floor((whole + (SUPER - 1)) * (1.0 / SUPER)), 1.0)
    d = [supers[:, 128 * k : 128 * k + 128].astype(BF) for k in range(3)]
    first = join(
        [
            times(d[0], 7),
            times(d[1], 7) + times(d[0], 8),
            times(d[2], 7) + times(d[1], 8) + times(d[0], 8),
        ]
    )
    lane = iota((8, n), 1)
    b = lane // per
    kind = jnp.where((b >= SIDE) & (b < SIDE + OWN), 0, 1)
    base = ((kind * per + lane % per) * PITCH).astype(F32)
    longest = jnp.broadcast_to(jnp.max(count, axis=1, keepdims=True), (8, n))
    row = iota((8, n), 0)
    info = jnp.zeros((8, n), F32)
    marked = jnp.max(jnp.max(line_ref[...], axis=1, keepdims=True), axis=0, keepdims=True)
    marked = jnp.broadcast_to(marked, (8, n))
    values = (source + base, first * SUPER + ahead, count, first, whole, supers, longest, marked)
    for k, value in enumerate(values):
        info = jnp.where(row == k, value, info)
    info_ref[...] = info.astype(I32)


def sort_groups(rec_ref, pos_ref, sorted_ref, groups):
    target = iota((GROUP, GROUP), 0).astype(F32).astype(BF)

    def body(g, carry):
        pos = jnp.broadcast_to(pos_ref[pl.ds(g, 1), :], (16, GROUP)).astype(BF)
        pos = jnp.concatenate([pos] * (GROUP // 16), axis=0)
        perm = jnp.where(pos == target, jnp.ones((), BF), jnp.zeros((), BF))
        sorted_ref[pl.ds(pl.multiple_of(g * PITCH, 8), GROUP), :] = nt(perm, rec_ref[g])
        return carry

    lax.fori_loop(0, groups, body, 0, unroll=16)


def join_runs(info, sorted_ref, rows_ref, n):
    def body(k, carry):
        rows_ref[pl.ds(info[1, k], STEP), :] = sorted_ref[pl.ds(info[0, k], STEP), :]
        return carry

    lax.fori_loop(0, n, body, 0, unroll=32)

    @pl.when(info[6, 0] > STEP)
    def _():
        def tail(k, carry):
            def one(r, c):
                rows_ref[pl.ds(info[1, k] + r, 1), :] = sorted_ref[pl.ds(info[0, k] + r, 1), :]
                return c

            lax.fori_loop(STEP, info[2, k], one, 0)
            return carry

        lax.fori_loop(0, n, tail, 0)


def make_columns(info, left_ref, rows_ref, cols_ref, per):
    def body(k, carry):
        at = pl.multiple_of(k * (BATCH * SUPER), BATCH * SUPER)
        got = nt(left_ref[...], rows_ref[pl.ds(at, BATCH * SUPER), :].astype(BF))
        for m in range(BATCH):
            cols_ref[k * BATCH + m] = got[:, m * SUPER : (m + 1) * SUPER]
        return carry

    lax.fori_loop(0, BUCKETS // BATCH, body, 0, unroll=6)
    last = (BUCKETS - 1) * per
    lax.fori_loop(BUCKETS // BATCH, (info[3, last] + info[5, last] + BATCH - 1) // BATCH, body, 0)


def deposit(info, cols_ref, grid_ref, acc_ref, per):
    lane = iota((1, SUPER), 1)
    pixels = iota((PX, SUPER), 0).astype(F32).astype(BF)
    lines = iota((SL_DEV, SUPER), 0).astype(F32).astype(BF)
    one, zero = jnp.ones((), BF), jnp.zeros((), BF)

    def packed(row):
        return jnp.broadcast_to(row, (16, SUPER)).astype(BF)

    def product(s, count):
        pixel = cols_ref[s, ION + 1 : ION + 2, :]
        pixel = jnp.where(lane < count, pixel - PX * jnp.floor(pixel * (1.0 / PX)), NOWHERE)
        here = packed(pixel) == pixels
        spread = [jnp.where(here, packed(cols_ref[s, i : i + 1, :]), zero) for i in range(ION)]
        line = jnp.concatenate([packed(cols_ref[s, ION : ION + 1, :])] * (SL_DEV // 16), axis=0)
        return nt(jnp.concatenate(spread, axis=0), jnp.where(line == lines, one, zero))

    def store(b, value):
        at = pl.ds(pl.multiple_of(b * PX, PX), PX)
        for i in range(ION):
            grid_ref[i, at, :] = value[i * PX : (i + 1) * PX].astype(BF)

    def body(b, carry):
        store(b, product(info[3, b * per], info[4, b * per]))
        return carry

    lax.fori_loop(0, BUCKETS, body, 0, unroll=12)

    last = (BUCKETS - 1) * per

    @pl.when(info[3, last] + info[5, last] > BUCKETS)
    def _():
        def again(b, carry):
            k = b * per

            @pl.when(info[5, k] > 1)
            def _():
                acc_ref[...] = jnp.zeros_like(acc_ref)

                def more(s, c):
                    acc_ref[...] += product(info[3, k] + s, info[4, k] - s * SUPER)
                    return c

                lax.fori_loop(0, info[5, k], more, 0)
                store(b, acc_ref[...])

            return carry

        lax.fori_loop(0, BUCKETS, again, 0)


def broaden(grid_ref, prof_ref, norm_ref, out_hbm, out_ref, sem):
    def body(q, carry):
        for j in range(QUAD):
            i = q * QUAD + j
            plane = grid_ref[i]
            norm = norm_ref[i, 0:1]
            out_ref[i, :, :128] = tn(plane[:256], prof_ref[i]) * norm
            out_ref[i, :, 128:] = tn(plane[128:], prof_ref[i]) * norm
            pltpu.make_async_copy(out_ref.at[i], out_hbm.at[i], sem).start()
        return carry

    lax.fori_loop(0, ION // QUAD, body, 0)
    pltpu.make_async_copy(out_ref, out_hbm, sem).wait()


def main_kernel(recv_ref, left_ref, norm_ref, scan_ref, tri_ref, prof_ref, out_hbm, again_ref, rec_ref, line_ref, pixel_ref,
                pos_ref, info_ref, sorted_ref, rows_ref, cols_ref, grid_ref, acc_ref, out_ref, info, sem, out_sem):
    groups = rec_ref.shape[0]
    per = groups // LISTS
    unpack(recv_ref, rec_ref, line_ref, pixel_ref, per)
    rank_slots(line_ref, pixel_ref, scan_ref, tri_ref, pos_ref, info_ref, per)
    to_scalars = pltpu.make_async_copy(info_ref, info, sem)
    to_scalars.start()
    sort_groups(rec_ref, pos_ref, sorted_ref, groups)
    to_scalars.wait()
    again_ref[0] = jnp.where(info[7, 0] >= MARK, 1, 0)
    join_runs(info, sorted_ref, rows_ref, BUCKETS * per)
    make_columns(info, left_ref, rows_ref, cols_ref, per)
    deposit(info, cols_ref, grid_ref, acc_ref, per)
    broaden(grid_ref, prof_ref, norm_ref, out_hbm, out_ref, out_sem)


def direct(abundances, sightline, pixel, counts, ion_table, doppler, lorentz_share):
    n_spec = lax.axis_size("spec")
    devices = lax.axis_size("los") * n_spec
    n_slots = abundances.shape[1]
    vmem = pl.BlockSpec(memory_space=pltpu.VMEM)
    smem = pl.BlockSpec(memory_space=pltpu.SMEM)
    anywhere = pl.BlockSpec(memory_space=pltpu.HBM)
    sent = pl.pallas_call(
        lambda *refs: pack_kernel(*refs, n_spec=n_spec),
        out_shape=jax.ShapeDtypeStruct((devices, LISTS * 8, 128), BF),
        in_specs=[anywhere] * 4,
        out_specs=anywhere,
        scratch_shapes=[
            pltpu.VMEM(abundances.shape, BF),
            pltpu.VMEM((n_slots // 128, 128), I32),
            pltpu.VMEM((n_slots // 128, 128), I32),
            pltpu.VMEM(counts.shape, I32),
            pltpu.VMEM((devices, LISTS * 8, 128), BF),
            pltpu.SemaphoreType.DMA((4,)),
            pltpu.SemaphoreType.DMA,
        ],
        compiler_params=pltpu.CompilerParams(vmem_limit_bytes=63 * 2**20),
        name="pack",
    )(abundances, sightline.reshape(n_slots // 128, 128), pixel.reshape(n_slots // 128, 128), counts)
    groups = LISTS * n_slots // GROUP
    n = BUCKETS * groups // LISTS
    table = jnp.pad(ion_table.T, ((0, 0), (0, VAL - ELEM)))
    prof, norm, left, scan, tri = pl.pallas_call(
        prepare_kernel,
        out_shape=[
            jax.ShapeDtypeStruct((ION, 4 * HW, 2 * HW), BF),
            jax.ShapeDtypeStruct((ION, 8, 2 * HW), F32),
            jax.ShapeDtypeStruct((OUTS, WIDE), BF),
            jax.ShapeDtypeStruct((9, 128, 128), BF),
            jax.ShapeDtypeStruct((GROUP, GROUP), BF),
        ],
        in_specs=[smem, smem, vmem],
        out_specs=[vmem] * 5,
        compiler_params=pltpu.CompilerParams(vmem_limit_bytes=10 * 2**20),
        cost_estimate=pl.CostEstimate(flops=20_000_000, bytes_accessed=4 * 2**20, transcendentals=3_000_000),
        name="prepare",
    )(doppler, lorentz_share, table)
    got = lax.all_to_all(sent, ("los", "spec"), split_axis=0, concat_axis=0, tiled=True)
    supers = LISTS * n_slots // SUPER + BUCKETS
    return pl.pallas_call(
        main_kernel,
        out_shape=[jax.ShapeDtypeStruct((ION, SL_DEV, PIX_DEV), F32), jax.ShapeDtypeStruct((1,), I32)],
        in_specs=[vmem] * 6,
        out_specs=[anywhere, smem],
        scratch_shapes=[
            pltpu.VMEM((groups, WIDE, GROUP), BF),
            pltpu.VMEM((groups, GROUP), F32),
            pltpu.VMEM((groups, GROUP), F32),
            pltpu.VMEM((groups, GROUP), F32),
            pltpu.VMEM((8, n), I32),
            pltpu.VMEM((groups * PITCH, WIDE), F32),
            pltpu.VMEM((supers * SUPER + STEP, WIDE), F32),
            pltpu.VMEM((supers, OUTS, SUPER), F32),
            pltpu.VMEM((ION, BUCKETS * PX, SL_DEV), BF),
            pltpu.VMEM((ION * PX, SL_DEV), F32),
            pltpu.VMEM((ION, SL_DEV, PIX_DEV), F32),
            pltpu.SMEM((8, n), I32),
            pltpu.SemaphoreType.DMA,
            pltpu.SemaphoreType.DMA,
        ],
        compiler_params=pltpu.CompilerParams(vmem_limit_bytes=46 * 2**20),
        name="deposit_broaden",
    )(got, left, norm, scan, tri, prof)


def with_halo(cells, sides, width):
    for axis, dim in sides:
        count = lax.axis_size(axis)
        head = lax.slice_in_dim(cells, 0, width, axis=dim)
        tail = lax.slice_in_dim(cells, cells.shape[dim] - width, cells.shape[dim], axis=dim)
        cells = jnp.concatenate(
            [
                lax.ppermute(tail, axis, [(i, (i + 1) % count) for i in range(count)]),
                cells,
                lax.ppermute(head, axis, [((i + 1) % count, i) for i in range(count)]),
            ],
            axis=dim,
        )
    return cells


def line_shape(offset, doppler, share):
    u = offset / doppler
    return (1.0 - share) * jnp.exp(-u * u) + share / (1.0 + u * u)


def deposit_onto(got_cols, line_rows, place, span):
    ions = got_cols.shape[0]
    n_rows = got_cols.shape[1]
    pixel_hot = (place[:, None] == lax.broadcasted_iota(jnp.int32, (1, span), 1)).astype(
        jnp.bfloat16
    )
    line_hot = (line_rows[None, :] == lax.broadcasted_iota(jnp.int32, (SL_DEV, 1), 0)).astype(
        jnp.bfloat16
    )
    group = 8
    grouped = got_cols.reshape(ions // group, group, n_rows)

    def deposit(part_cols):
        spread = (part_cols[:, None, :] * line_hot[None, :, :]).reshape(group * SL_DEV, n_rows)
        return jnp.dot(spread, pixel_hot, preferred_element_type=jnp.float32).reshape(
            group, SL_DEV, span
        )

    return lax.map(deposit, grouped).reshape(ions, SL_DEV, span)


def broaden_window(padded, pix_dev, width, share, norm):
    inner = lax.broadcasted_iota(jnp.int32, (pix_dev + 2 * HW, pix_dev), 0)
    outer = lax.broadcasted_iota(jnp.int32, (pix_dev + 2 * HW, pix_dev), 1)
    delta = (outer + HW - inner).astype(jnp.float32)[None, :, :]
    matrix = jnp.where(jnp.abs(delta) <= HW, line_shape(delta, width, share), 0.0) / norm
    return jnp.einsum("isk,ikj->isj", padded, matrix, precision=lax.Precision.HIGHEST)


def general(abundances, sightline, pixel, counts, ion_table, doppler, lorentz_share):
    n_los = lax.axis_size("los")
    n_spec = lax.axis_size("spec")
    devices = n_los * n_spec
    n_slots = abundances.shape[1]
    slots = n_slots // devices
    pix_dev = PIXELS // n_spec
    columns = jnp.dot(ion_table.T, abundances.astype(jnp.float32), precision=lax.Precision.HIGHEST)
    live = lax.broadcasted_iota(jnp.int32, (devices, slots), 1) < counts[0][:, None]
    columns = jnp.where(live.reshape(1, n_slots), columns, 0.0).astype(jnp.bfloat16)
    cell = (sightline * pix_dev + pixel).reshape(1, n_slots)
    got_cols, got_cell = (
        lax.all_to_all(columns, ("los", "spec"), split_axis=1, concat_axis=1, tiled=True),
        lax.all_to_all(cell, ("los", "spec"), split_axis=1, concat_axis=1, tiled=True),
    )
    got_cell = got_cell.reshape(n_slots)
    grid = deposit_onto(got_cols, got_cell // pix_dev, got_cell % pix_dev, pix_dev)
    offsets = jnp.arange(-HW, HW + 1).astype(jnp.float32)
    totals = jnp.sum(line_shape(offsets[None, :], doppler[:, None], lorentz_share[:, None]), axis=1)
    width = doppler[:, None, None]
    share = lorentz_share[:, None, None]
    norm = totals[:, None, None]
    padded = with_halo(grid, (("spec", 2),), HW)
    depth = broaden_window(padded, pix_dev, width, share, norm)
    return depth


def on_device(*args):
    depth, again = direct(*args)
    return lax.fori_loop(0, again[0], lambda _, old: general(*args), depth)


def solution(mesh):
    in_specs = (
        P(None, ("los", "spec")),
        P(("los", "spec")),
        P(("los", "spec")),
        P(("los", "spec"), None),
        P(),
        P(),
        P(),
    )
    return jax.shard_map(
        on_device, mesh=mesh, in_specs=in_specs, out_specs=P(None, "los", "spec"), check_vma=False
    )
```

```python
import jax
import jax.numpy as jnp
from jax import lax
from jax.experimental import pallas as pl
from jax.experimental.pallas import tpu as pltpu
from jax.sharding import PartitionSpec as P

ELEM = 30
ION = 32
VAL = 32
WIDE = 3 * VAL
OUTS = ION + 16
BATCH = 4
HW = 64
SL_DEV = 256
PIX_DEV = 256
PIXELS = 4096
CAP = 32
DEAD = 256.0
MARK = 384.0
NOWHERE = 512.0
LISTS = 2
GROUP = 256
SUPER = 256
PX = 16
SIDE = HW // PX
OWN = PIX_DEV // PX
BUCKETS = OWN + 2 * SIDE
SHARED = 0.15
QUAD = 16
STEP = 32
PITCH = GROUP + STEP
SENT_TILES = 2
BF = jnp.bfloat16
F32 = jnp.float32
I32 = jnp.int32


def iota(shape, dim):
    return lax.broadcasted_iota(I32, shape, dim)


def nt(a, b):
    return lax.dot_general(a, b, (((1,), (1,)), ((), ())), preferred_element_type=F32)


def tn(a, b):
    return lax.dot_general(a, b, (((0,), (0,)), ((), ())), preferred_element_type=F32)


def swap_blocks(tiles):
    lane = iota((8, 128), 1)
    low = lane < 64
    even = (lane // 32) % 2 == 0
    far = [pltpu.roll(t, 64, 1) for t in tiles]
    half = [
        jnp.where(low, tiles[0], far[2]),
        jnp.where(low, tiles[1], far[3]),
        jnp.where(low, far[0], tiles[2]),
        jnp.where(low, far[1], tiles[3]),
    ]
    out = [None] * 4
    for p in (0, 2):
        a, b = half[p], half[p + 1]
        out[p] = jnp.where(even, a, pltpu.roll(b, 32, 1))
        out[p + 1] = jnp.where(even, pltpu.roll(a, 96, 1), b)
    return out


def pack_kernel(abund_hbm, line_hbm, pixel_hbm, counts_hbm, out_hbm, abund_ref, line_ref, pixel_ref, counts_ref,
                out_ref, sems, out_sem, *, n_spec):
    copies = [
        pltpu.make_async_copy(src, dst, sems.at[k])
        for k, (src, dst) in enumerate(
            ((counts_hbm, counts_ref), (line_hbm, line_ref), (pixel_hbm, pixel_ref), (abund_hbm, abund_ref))
        )
    ]
    for copy in copies:
        copy.start()
    devices = counts_ref.shape[1]
    quads = devices // 4
    per_tile = n_spec // 4
    one = lambda m: jnp.where(m, 1.0, 0.0).astype(BF)
    dot = lambda a, b: jnp.dot(a, b, preferred_element_type=F32)
    x, y = iota((128, 128), 0), iota((128, 128), 1)
    same = x // CAP == y // CAP
    lane = iota((quads, 128), 1)
    row = iota((quads, 128), 0)
    slot = (lane % CAP).astype(F32)
    pick = one(iota((devices, 128), 0) % 4 == iota((devices, 128), 1) // CAP)
    for copy in copies[:3]:
        copy.wait()
    owner = iota((quads, devices), 1) // 4 == iota((quads, devices), 0)
    live = slot < dot(jnp.where(owner, counts_ref[...].astype(F32), 0.0).astype(BF), pick)
    line = jnp.where(live, line_ref[...].astype(F32), DEAD)
    pixel = pixel_ref[...].astype(F32)

    low = jnp.where(live & (pixel < HW), 1.0, 0.0)
    high = jnp.where(live & (pixel >= PIX_DEV - HW), 1.0, 0.0)
    marks = jnp.concatenate([low, 1.0 - low - high, high], axis=0).astype(BF)
    rank = dot(marks, one(same & (x < y)))
    total = dot(marks, one(same))
    n_low, n_high = total[:quads], total[2 * quads :]
    place = jnp.where(high > 0, CAP - n_high + rank[2 * quads :], n_low + rank[quads : 2 * quads])
    place = jnp.where(low > 0, rank[:quads], place) + (lane // CAP * CAP).astype(F32)
    ends = jnp.concatenate([n_low, n_high], axis=0).astype(BF)
    ends = [dot(ends, one(x == CAP * b)) for b in range(4)]
    lows = [e[:quads] for e in ends]
    highs = [e[quads:] for e in ends]

    def turn(v, ahead):
        near, far = (quads - 1, per_tile - 1) if ahead else (1, quads - per_tile + 1)
        edge = row % per_tile == (per_tile - 1 if ahead else 0)
        return jnp.where(edge, pltpu.roll(v, far, 0), pltpu.roll(v, near, 0))

    used = [lows[1] + turn(highs[3], False), lows[2] + highs[0], lows[3] + highs[1], turn(lows[0], True) + highs[2]]
    used = jnp.maximum(jnp.maximum(used[0], used[1]), jnp.maximum(used[2], used[3]))
    line = jnp.where(jnp.max(used, axis=0, keepdims=True) > CAP, MARK, line)

    target = x.astype(F32).astype(BF)
    spot = (iota((8, 128), 1) % CAP).astype(F32)
    hole = (iota((8, 128), 0) == ELEM % 8) & (iota((8, 128), 1) // CAP == ELEM // 8)
    hole = jnp.where(hole, DEAD, 0.0)
    copies[3].wait()
    for t in range(devices // n_spec):
        msgs = []
        for a in range(t * per_tile, (t + 1) * per_tile):
            ab = abund_ref[:, a * 128 : (a + 1) * 128].astype(F32)
            vals = jnp.concatenate([ab, line[a : a + 1], pixel[a : a + 1]], axis=0).astype(BF)
            dest = jnp.broadcast_to(place[a : a + 1], (16, 128)).astype(BF)
            dest = jnp.concatenate([dest] * 8, axis=0)
            moved = nt(vals, jnp.where(dest == target, jnp.ones((), BF), jnp.zeros((), BF)))
            msgs += swap_blocks([moved[8 * j : 8 * j + 8] for j in range(4)])
        for c in range(n_spec):
            prev, after = (c - 1) % n_spec, (c + 1) % n_spec
            run = lambda v, k: v[k % 4][t * per_tile + k // 4 : t * per_tile + k // 4 + 1]
            halo = jnp.where(spot >= CAP - run(highs, prev), msgs[prev], hole)
            halo = jnp.where(spot < run(lows, after), msgs[after], halo)
            out_ref[t * n_spec + c] = jnp.concatenate([msgs[c], halo], axis=0).astype(BF)
        if (t + 1) % SENT_TILES == 0:
            part = pl.ds((t + 1 - SENT_TILES) * n_spec, SENT_TILES * n_spec)
            pltpu.make_async_copy(out_ref.at[part], out_hbm.at[part], out_sem).start()
    pltpu.make_async_copy(out_ref, out_hbm, out_sem).wait()


def prepare_kernel(doppler_ref, share_ref, table_ref, prof_ref, norm_ref, left_ref, scan_ref, tri_ref):
    offset = iota((4 * HW, 2 * HW), 1) + HW - iota((4 * HW, 2 * HW), 0)
    near = jnp.abs(offset) <= HW
    offset = offset.astype(F32)
    left_of = iota((2 * HW, 2 * HW), 1) <= iota((2 * HW, 2 * HW), 0)

    def body(i, carry):
        share = share_ref[i]
        u = offset / doppler_ref[i]
        raw = (1.0 - share) * jnp.exp(-u * u) + share / (1.0 + u * u)
        raw = jnp.where(near, raw, 0.0)
        norm_ref[i] = jnp.broadcast_to(1.0 / jnp.sum(raw, axis=0, keepdims=True), (8, 2 * HW))
        raw = jnp.where(left_of, raw[: 2 * HW], raw[2 * HW :])
        top = raw.astype(BF)
        prof_ref[i] = jnp.concatenate([top, (raw - top.astype(F32)).astype(BF)], axis=1)
        return carry

    lax.fori_loop(0, ION, body, 0)

    table = table_ref[...]
    hi = table.astype(BF)
    rest = table - hi.astype(F32)
    mid = rest.astype(BF)
    low = (rest - mid.astype(F32)).astype(BF)
    picks = jnp.where(iota((16, WIDE), 1) == iota((16, WIDE), 0) + ELEM, 1.0, 0.0)
    picks = jnp.where(iota((16, WIDE), 0) < 2, picks, 0.0).astype(BF)
    left_ref[...] = jnp.concatenate([jnp.concatenate([hi, mid, low], axis=1), picks], axis=0)

    x, y = iota((128, 128), 0), iota((128, 128), 1)
    one = lambda m: jnp.where(m, 1.0, 0.0).astype(BF)
    bucket, group, half = x // 16 == y // 16, x % 16 == y % 16, x // 64 == y // 64
    for k, m in enumerate(
        (
            bucket & (x < y),
            bucket,
            group & half & (x < y),
            group & (x < y),
            group & (x >= 64),
            group & (y < 64),
            group & (x // 64 != y // 64),
            (x % 16 == 0) & (x // 16 < y // 16),
            x % 16 == 0,
        )
    ):
        scan_ref[k] = one(m)
    tri_ref[...] = one(iota((GROUP, GROUP), 0) < iota((GROUP, GROUP), 1))


def unpack(recv_ref, rec_ref, line_ref, pixel_ref, per):
    def body(g, carry):
        tiles = [recv_ref[g * 8 + p].astype(F32) for p in range(8)]
        for kind in range(LISTS):
            halves = []
            for h in range(2):
                srcs = [tiles[4 * h + s][8 * kind : 8 * kind + 8] for s in range(4)]
                halves.append(jnp.concatenate(swap_blocks(srcs), axis=0))
            rec = jnp.concatenate(halves, axis=1)
            rec_ref[kind * per + g] = jnp.concatenate([rec.astype(BF)] * 3, axis=0)
            line_ref[pl.ds(kind * per + g, 1), :] = rec[ELEM : ELEM + 1]
            pixel_ref[pl.ds(kind * per + g, 1), :] = rec[ELEM + 1 : ELEM + 2]
        return carry

    lax.fori_loop(0, per, body, 0, unroll=4)


def rank_slots(line_ref, pixel_ref, scan_ref, tri_ref, pos_ref, info_ref, per):
    live = line_ref[...] < SL_DEV
    block = jnp.where(live, jnp.floor(pixel_ref[...] * (1.0 / PX)), -1.0)
    marks = []
    for b in range(BUCKETS):
        if b < SIDE:
            kind, which = 1, OWN - SIDE + b
        elif b < SIDE + OWN:
            kind, which = 0, b - SIDE
        else:
            kind, which = 1, b - SIDE - OWN
        marks.append(jnp.where(block[kind * per : (kind + 1) * per] == which, 1.0, 0.0).astype(BF))
    marks = jnp.concatenate(marks, axis=0)
    n = BUCKETS * per
    rank = jnp.dot(marks, tri_ref[...], preferred_element_type=F32)
    total = jnp.dot(marks, jnp.ones((GROUP, GROUP), BF), preferred_element_type=F32)
    count = nt(jnp.ones((8, GROUP), BF), marks)
    sides = [*range(SIDE), *range(SIDE + OWN, BUCKETS)]
    for kind, buckets in enumerate((range(SIDE, SIDE + OWN), sides)):
        start = jnp.zeros((per, GROUP), F32)
        place = jnp.zeros((per, GROUP), F32)
        used = jnp.zeros((per, GROUP), F32)
        for b in buckets:
            rows = slice(b * per, (b + 1) * per)
            mark = marks[rows].astype(F32)
            place = place + mark * (start + rank[rows])
            used = used + mark
            start = start + total[rows]
        pos_ref[kind * per : (kind + 1) * per] = jnp.where(used > 0, place, NOWHERE)
    times = lambda a, k: jnp.dot(a, scan_ref[k], preferred_element_type=F32)
    join = lambda a: jnp.concatenate(a, axis=1)
    c = [count[:, 128 * k : 128 * k + 128].astype(BF) for k in range(3)]
    ahead, whole = (join([times(a, k) for a in c]) for k in (0, 1))
    source = join(
        [
            times(c[0], 2),
            times(c[1], 3) + times(c[0], 4),
            times(c[2], 2) + times(c[1], 5) + times(c[0], 6),
        ]
    )
    supers = jnp.maximum(jnp.floor((whole + (SUPER - 1)) * (1.0 / SUPER)), 1.0)
    d = [supers[:, 128 * k : 128 * k + 128].astype(BF) for k in range(3)]
    first = join(
        [
            times(d[0], 7),
            times(d[1], 7) + times(d[0], 8),
            times(d[2], 7) + times(d[1], 8) + times(d[0], 8),
        ]
    )
    lane = iota((8, n), 1)
    b = lane // per
    kind = jnp.where((b >= SIDE) & (b < SIDE + OWN), 0, 1)
    base = ((kind * per + lane % per) * PITCH).astype(F32)
    longest = jnp.broadcast_to(jnp.max(count, axis=1, keepdims=True), (8, n))
    row = iota((8, n), 0)
    info = jnp.zeros((8, n), F32)
    marked = jnp.max(jnp.max(line_ref[...], axis=1, keepdims=True), axis=0, keepdims=True)
    marked = jnp.broadcast_to(marked, (8, n))
    values = (source + base, first * SUPER + ahead, count, first, whole, supers, longest, marked)
    for k, value in enumerate(values):
        info = jnp.where(row == k, value, info)
    info_ref[...] = info.astype(I32)


def sort_groups(rec_ref, pos_ref, sorted_ref, groups):
    target = iota((GROUP, GROUP), 0).astype(F32).astype(BF)

    def body(g, carry):
        pos = jnp.broadcast_to(pos_ref[pl.ds(g, 1), :], (16, GROUP)).astype(BF)
        pos = jnp.concatenate([pos] * (GROUP // 16), axis=0)
        perm = jnp.where(pos == target, jnp.ones((), BF), jnp.zeros((), BF))
        sorted_ref[pl.ds(pl.multiple_of(g * PITCH, 8), GROUP), :] = nt(perm, rec_ref[g])
        return carry

    lax.fori_loop(0, groups, body, 0, unroll=16)


def join_runs(info, sorted_ref, rows_ref, n):
    def body(k, carry):
        rows_ref[pl.ds(info[1, k], STEP), :] = sorted_ref[pl.ds(info[0, k], STEP), :]
        return carry

    lax.fori_loop(0, n, body, 0, unroll=32)

    @pl.when(info[6, 0] > STEP)
    def _():
        def tail(k, carry):
            def one(r, c):
                rows_ref[pl.ds(info[1, k] + r, 1), :] = sorted_ref[pl.ds(info[0, k] + r, 1), :]
                return c

            lax.fori_loop(STEP, info[2, k], one, 0)
            return carry

        lax.fori_loop(0, n, tail, 0)


def make_columns(info, left_ref, rows_ref, cols_ref, per):
    def body(k, carry):
        at = pl.multiple_of(k * (BATCH * SUPER), BATCH * SUPER)
        got = nt(left_ref[...], rows_ref[pl.ds(at, BATCH * SUPER), :].astype(BF))
        for m in range(BATCH):
            cols_ref[k * BATCH + m] = got[:, m * SUPER : (m + 1) * SUPER]
        return carry

    lax.fori_loop(0, BUCKETS // BATCH, body, 0, unroll=6)
    last = (BUCKETS - 1) * per
    lax.fori_loop(BUCKETS // BATCH, (info[3, last] + info[5, last] + BATCH - 1) // BATCH, body, 0)


def deposit(info, cols_ref, grid_ref, low_ref, acc_ref, energy_ref, per):
    lane = iota((1, SUPER), 1)
    pixels = iota((PX, SUPER), 0).astype(F32).astype(BF)
    lines = iota((SL_DEV, SUPER), 0).astype(F32).astype(BF)
    one, zero = jnp.ones((), BF), jnp.zeros((), BF)
    last = (BUCKETS - 1) * per
    crowded = info[3, last] + info[5, last] > BUCKETS

    def packed(row):
        return jnp.broadcast_to(row, (16, SUPER)).astype(BF)

    def product(s, count):
        pixel = cols_ref[s, ION + 1 : ION + 2, :]
        pixel = jnp.where(lane < count, pixel - PX * jnp.floor(pixel * (1.0 / PX)), NOWHERE)
        here = packed(pixel) == pixels
        cols = cols_ref[s, :ION, :]
        size = jnp.sqrt(jnp.sum(cols * cols, axis=0, keepdims=True))
        spread = [jnp.where(here, packed(cols_ref[s, i : i + 1, :]), zero) for i in range(ION)]
        spread += [jnp.where(here, packed(size), zero), jnp.where(here, one, zero)]
        line = jnp.concatenate([packed(cols_ref[s, ION : ION + 1, :])] * (SL_DEV // 16), axis=0)
        return nt(jnp.concatenate(spread, axis=0), jnp.where(line == lines, one, zero))

    def place(b):
        return pl.ds(pl.multiple_of(b * PX, PX), PX)

    energy_ref[...] = jnp.zeros_like(energy_ref)

    def body(b, carry):
        value = product(info[3, b * per], info[4, b * per])
        for i in range(ION):
            grid_ref[i, place(b), :] = value[i * PX : (i + 1) * PX].astype(BF)
        energy = value[ION * PX : (ION + 1) * PX]
        energy = energy * energy
        energy_ref[0] += energy
        energy_ref[1] += jnp.where(value[(ION + 1) * PX :] > 1.5, energy, 0.0)
        return carry

    lax.fori_loop(0, BUCKETS, body, 0, unroll=12)
    fine = crowded | (jnp.sum(energy_ref[1]) > SHARED * jnp.sum(energy_ref[0]))

    @pl.when(fine)
    def _():
        def again(b, carry):
            k = b * per
            acc_ref[...] = jnp.zeros_like(acc_ref)

            def more(s, c):
                acc_ref[...] += product(info[3, k] + s, info[4, k] - s * SUPER)
                return c

            lax.fori_loop(0, info[5, k], more, 0)
            for i in range(ION):
                value = acc_ref[i * PX : (i + 1) * PX, :]
                top = value.astype(BF)
                grid_ref[i, place(b), :] = top
                low_ref[i, place(b), :] = (value - top.astype(F32)).astype(BF)
            return carry

        lax.fori_loop(0, BUCKETS, again, 0)

    return fine


def broaden(grid_ref, low_ref, fine, prof_ref, norm_ref, out_hbm, out_ref, sem):
    row, col = iota((2 * HW, 4 * HW), 0), iota((2 * HW, 4 * HW), 1) % (2 * HW)
    zero = jnp.zeros((), F32)
    upper, lower = (jnp.where(m, 1.0, zero).astype(BF) > jnp.zeros((), BF) for m in (col <= row, col >= row))

    def halves(planes, i, at):
        shape = prof_ref[i]
        shape = jnp.concatenate([jnp.where(m, shape, jnp.zeros((), BF)) for m in (upper, lower)], axis=0)
        both = sum(tn(p[at : at + 4 * HW], shape) for p in planes)
        return (both[:, : 2 * HW] + both[:, 2 * HW :]) * norm_ref[i, 0:1]

    def run(refs, unroll):
        def body(q, carry):
            for j in range(unroll):
                i = q * unroll + j
                planes = [ref[i] for ref in refs]
                out_ref[i, :, :128] = halves(planes, i, 0)
                out_ref[i, :, 128:] = halves(planes, i, 2 * HW)
                pltpu.make_async_copy(out_ref.at[i], out_hbm.at[i], sem).start()
            return carry

        lax.fori_loop(0, ION // unroll, body, 0)

    @pl.when(fine)
    def _():
        run((grid_ref, low_ref), 1)

    @pl.when(jnp.logical_not(fine))
    def _():
        run((grid_ref,), QUAD)

    pltpu.make_async_copy(out_ref, out_hbm, sem).wait()


def main_kernel(recv_ref, left_ref, norm_ref, scan_ref, tri_ref, prof_ref, out_hbm, again_ref, rec_ref, line_ref, pixel_ref,
                pos_ref, info_ref, sorted_ref, rows_ref, cols_ref, grid_ref, low_ref, acc_ref, energy_ref, out_ref, info, sem,
                out_sem):
    groups = rec_ref.shape[0]
    per = groups // LISTS
    unpack(recv_ref, rec_ref, line_ref, pixel_ref, per)
    rank_slots(line_ref, pixel_ref, scan_ref, tri_ref, pos_ref, info_ref, per)
    to_scalars = pltpu.make_async_copy(info_ref, info, sem)
    to_scalars.start()
    sort_groups(rec_ref, pos_ref, sorted_ref, groups)
    to_scalars.wait()
    again_ref[0] = jnp.where(info[7, 0] >= MARK, 1, 0)
    join_runs(info, sorted_ref, rows_ref, BUCKETS * per)
    make_columns(info, left_ref, rows_ref, cols_ref, per)
    fine = deposit(info, cols_ref, grid_ref, low_ref, acc_ref, energy_ref, per)
    broaden(grid_ref, low_ref, fine, prof_ref, norm_ref, out_hbm, out_ref, out_sem)


def direct(abundances, sightline, pixel, counts, ion_table, doppler, lorentz_share):
    n_spec = lax.axis_size("spec")
    devices = lax.axis_size("los") * n_spec
    n_slots = abundances.shape[1]
    vmem = pl.BlockSpec(memory_space=pltpu.VMEM)
    smem = pl.BlockSpec(memory_space=pltpu.SMEM)
    anywhere = pl.BlockSpec(memory_space=pltpu.HBM)
    sent = pl.pallas_call(
        lambda *refs: pack_kernel(*refs, n_spec=n_spec),
        out_shape=jax.ShapeDtypeStruct((devices, LISTS * 8, 128), BF),
        in_specs=[anywhere] * 4,
        out_specs=anywhere,
        scratch_shapes=[
            pltpu.VMEM(abundances.shape, BF),
            pltpu.VMEM((n_slots // 128, 128), I32),
            pltpu.VMEM((n_slots // 128, 128), I32),
            pltpu.VMEM(counts.shape, I32),
            pltpu.VMEM((devices, LISTS * 8, 128), BF),
            pltpu.SemaphoreType.DMA((4,)),
            pltpu.SemaphoreType.DMA,
        ],
        compiler_params=pltpu.CompilerParams(vmem_limit_bytes=63 * 2**20),
        name="pack",
    )(abundances, sightline.reshape(n_slots // 128, 128), pixel.reshape(n_slots // 128, 128), counts)
    groups = LISTS * n_slots // GROUP
    n = BUCKETS * groups // LISTS
    table = jnp.pad(ion_table.T, ((0, 0), (0, VAL - ELEM)))
    prof, norm, left, scan, tri = pl.pallas_call(
        prepare_kernel,
        out_shape=[
            jax.ShapeDtypeStruct((ION, 2 * HW, 4 * HW), BF),
            jax.ShapeDtypeStruct((ION, 8, 2 * HW), F32),
            jax.ShapeDtypeStruct((OUTS, WIDE), BF),
            jax.ShapeDtypeStruct((9, 128, 128), BF),
            jax.ShapeDtypeStruct((GROUP, GROUP), BF),
        ],
        in_specs=[smem, smem, vmem],
        out_specs=[vmem] * 5,
        compiler_params=pltpu.CompilerParams(vmem_limit_bytes=10 * 2**20),
        cost_estimate=pl.CostEstimate(flops=20_000_000, bytes_accessed=4 * 2**20, transcendentals=3_000_000),
        name="prepare",
    )(doppler, lorentz_share, table)
    got = lax.all_to_all(sent, ("los", "spec"), split_axis=0, concat_axis=0, tiled=True)
    supers = LISTS * n_slots // SUPER + BUCKETS
    return pl.pallas_call(
        main_kernel,
        out_shape=[jax.ShapeDtypeStruct((ION, SL_DEV, PIX_DEV), F32), jax.ShapeDtypeStruct((1,), I32)],
        in_specs=[vmem] * 6,
        out_specs=[anywhere, smem],
        scratch_shapes=[
            pltpu.VMEM((groups, WIDE, GROUP), BF),
            pltpu.VMEM((groups, GROUP), F32),
            pltpu.VMEM((groups, GROUP), F32),
            pltpu.VMEM((groups, GROUP), F32),
            pltpu.VMEM((8, n), I32),
            pltpu.VMEM((groups * PITCH, WIDE), F32),
            pltpu.VMEM((supers * SUPER + STEP, WIDE), F32),
            pltpu.VMEM((supers, OUTS, SUPER), F32),
            pltpu.VMEM((ION, BUCKETS * PX, SL_DEV), BF),
            pltpu.VMEM((ION, BUCKETS * PX, SL_DEV), BF),
            pltpu.VMEM(((ION + 2) * PX, SL_DEV), F32),
            pltpu.VMEM((2, PX, SL_DEV), F32),
            pltpu.VMEM((ION, SL_DEV, PIX_DEV), F32),
            pltpu.SMEM((8, n), I32),
            pltpu.SemaphoreType.DMA,
            pltpu.SemaphoreType.DMA,
        ],
        compiler_params=pltpu.CompilerParams(vmem_limit_bytes=41 * 2**20),
        name="deposit_broaden",
    )(got, left, norm, scan, tri, prof)


def with_halo(cells, sides, width):
    for axis, dim in sides:
        count = lax.axis_size(axis)
        head = lax.slice_in_dim(cells, 0, width, axis=dim)
        tail = lax.slice_in_dim(cells, cells.shape[dim] - width, cells.shape[dim], axis=dim)
        cells = jnp.concatenate(
            [
                lax.ppermute(tail, axis, [(i, (i + 1) % count) for i in range(count)]),
                cells,
                lax.ppermute(head, axis, [((i + 1) % count, i) for i in range(count)]),
            ],
            axis=dim,
        )
    return cells


def line_shape(offset, doppler, share):
    u = offset / doppler
    return (1.0 - share) * jnp.exp(-u * u) + share / (1.0 + u * u)


def deposit_onto(got_cols, line_rows, place, span):
    ions = got_cols.shape[0]
    n_rows = got_cols.shape[1]
    pixel_hot = (place[:, None] == lax.broadcasted_iota(jnp.int32, (1, span), 1)).astype(
        jnp.bfloat16
    )
    line_hot = (line_rows[None, :] == lax.broadcasted_iota(jnp.int32, (SL_DEV, 1), 0)).astype(
        jnp.bfloat16
    )
    group = 8
    grouped = got_cols.reshape(ions // group, group, n_rows)

    def deposit(part_cols):
        spread = (part_cols[:, None, :] * line_hot[None, :, :]).reshape(group * SL_DEV, n_rows)
        return jnp.dot(spread, pixel_hot, preferred_element_type=jnp.float32).reshape(
            group, SL_DEV, span
        )

    return lax.map(deposit, grouped).reshape(ions, SL_DEV, span)


def broaden_window(padded, pix_dev, width, share, norm):
    inner = lax.broadcasted_iota(jnp.int32, (pix_dev + 2 * HW, pix_dev), 0)
    outer = lax.broadcasted_iota(jnp.int32, (pix_dev + 2 * HW, pix_dev), 1)
    delta = (outer + HW - inner).astype(jnp.float32)[None, :, :]
    matrix = jnp.where(jnp.abs(delta) <= HW, line_shape(delta, width, share), 0.0) / norm
    return jnp.einsum("isk,ikj->isj", padded, matrix, precision=lax.Precision.HIGHEST)


def general(abundances, sightline, pixel, counts, ion_table, doppler, lorentz_share):
    n_los = lax.axis_size("los")
    n_spec = lax.axis_size("spec")
    devices = n_los * n_spec
    n_slots = abundances.shape[1]
    slots = n_slots // devices
    pix_dev = PIXELS // n_spec
    columns = jnp.dot(ion_table.T, abundances.astype(jnp.float32), precision=lax.Precision.HIGHEST)
    live = lax.broadcasted_iota(jnp.int32, (devices, slots), 1) < counts[0][:, None]
    columns = jnp.where(live.reshape(1, n_slots), columns, 0.0).astype(jnp.bfloat16)
    cell = (sightline * pix_dev + pixel).reshape(1, n_slots)
    got_cols, got_cell = (
        lax.all_to_all(columns, ("los", "spec"), split_axis=1, concat_axis=1, tiled=True),
        lax.all_to_all(cell, ("los", "spec"), split_axis=1, concat_axis=1, tiled=True),
    )
    got_cell = got_cell.reshape(n_slots)
    grid = deposit_onto(got_cols, got_cell // pix_dev, got_cell % pix_dev, pix_dev)
    offsets = jnp.arange(-HW, HW + 1).astype(jnp.float32)
    totals = jnp.sum(line_shape(offsets[None, :], doppler[:, None], lorentz_share[:, None]), axis=1)
    width = doppler[:, None, None]
    share = lorentz_share[:, None, None]
    norm = totals[:, None, None]
    padded = with_halo(grid, (("spec", 2),), HW)
    depth = broaden_window(padded, pix_dev, width, share, norm)
    return depth


def on_device(*args):
    depth, again = direct(*args)
    return lax.fori_loop(0, again[0], lambda _, old: general(*args), depth)


def solution(mesh):
    in_specs = (
        P(None, ("los", "spec")),
        P(("los", "spec")),
        P(("los", "spec")),
        P(("los", "spec"), None),
        P(),
        P(),
        P(),
    )
    return jax.shard_map(
        on_device, mesh=mesh, in_specs=in_specs, out_specs=P(None, "los", "spec"), check_vma=False
    )
```

```python
import jax
import jax.numpy as jnp
from jax import lax
from jax.experimental import pallas as pl
from jax.experimental.pallas import tpu as pltpu
from jax.sharding import PartitionSpec as P

ELEM = 30
ION = 32
VAL = 32
WIDE = 3 * VAL
OUTS = ION + 16
BATCH = 4
HW = 64
SL_DEV = 256
PIX_DEV = 256
PIXELS = 4096
CAP = 32
DEAD = 256.0
MARK = 384.0
NOWHERE = 512.0
LISTS = 2
GROUP = 256
SUPER = 256
PX = 16
SIDE = HW // PX
OWN = PIX_DEV // PX
BUCKETS = OWN + 2 * SIDE
SHARED = 0.15
QUAD = 16
STEP = 32
PITCH = GROUP + STEP
SENT_TILES = 2
BF = jnp.bfloat16
F32 = jnp.float32
I32 = jnp.int32


def iota(shape, dim):
    return lax.broadcasted_iota(I32, shape, dim)


def nt(a, b):
    return lax.dot_general(a, b, (((1,), (1,)), ((), ())), preferred_element_type=F32)


def tn(a, b):
    return lax.dot_general(a, b, (((0,), (0,)), ((), ())), preferred_element_type=F32)


def swap_blocks(tiles):
    lane = iota((8, 128), 1)
    low = lane < 64
    even = (lane // 32) % 2 == 0
    far = [pltpu.roll(t, 64, 1) for t in tiles]
    half = [
        jnp.where(low, tiles[0], far[2]),
        jnp.where(low, tiles[1], far[3]),
        jnp.where(low, far[0], tiles[2]),
        jnp.where(low, far[1], tiles[3]),
    ]
    out = [None] * 4
    for p in (0, 2):
        a, b = half[p], half[p + 1]
        out[p] = jnp.where(even, a, pltpu.roll(b, 32, 1))
        out[p + 1] = jnp.where(even, pltpu.roll(a, 96, 1), b)
    return out


def pack_kernel(abund_hbm, line_hbm, pixel_hbm, counts_hbm, out_hbm, abund_ref, line_ref, pixel_ref, counts_ref,
                out_ref, sems, out_sem, *, n_spec):
    copies = [
        pltpu.make_async_copy(src, dst, sems.at[k])
        for k, (src, dst) in enumerate(
            ((counts_hbm, counts_ref), (line_hbm, line_ref), (pixel_hbm, pixel_ref), (abund_hbm, abund_ref))
        )
    ]
    for copy in copies:
        copy.start()
    devices = counts_ref.shape[1]
    quads = devices // 4
    per_tile = n_spec // 4
    one = lambda m: jnp.where(m, 1.0, 0.0).astype(BF)
    dot = lambda a, b: jnp.dot(a, b, preferred_element_type=F32)
    x, y = iota((128, 128), 0), iota((128, 128), 1)
    same = x // CAP == y // CAP
    lane = iota((quads, 128), 1)
    row = iota((quads, 128), 0)
    slot = (lane % CAP).astype(F32)
    pick = one(iota((devices, 128), 0) % 4 == iota((devices, 128), 1) // CAP)
    for copy in copies[:3]:
        copy.wait()
    owner = iota((quads, devices), 1) // 4 == iota((quads, devices), 0)
    live = slot < dot(jnp.where(owner, counts_ref[...].astype(F32), 0.0).astype(BF), pick)
    line = jnp.where(live, line_ref[...].astype(F32), DEAD)
    pixel = pixel_ref[...].astype(F32)

    low = jnp.where(live & (pixel < HW), 1.0, 0.0)
    high = jnp.where(live & (pixel >= PIX_DEV - HW), 1.0, 0.0)
    marks = jnp.concatenate([low, 1.0 - low - high, high], axis=0).astype(BF)
    rank = dot(marks, one(same & (x < y)))
    total = dot(marks, one(same))
    n_low, n_high = total[:quads], total[2 * quads :]
    place = jnp.where(high > 0, CAP - n_high + rank[2 * quads :], n_low + rank[quads : 2 * quads])
    place = jnp.where(low > 0, rank[:quads], place) + (lane // CAP * CAP).astype(F32)
    ends = jnp.concatenate([n_low, n_high], axis=0).astype(BF)
    ends = [dot(ends, one(x == CAP * b)) for b in range(4)]
    lows = [e[:quads] for e in ends]
    highs = [e[quads:] for e in ends]

    def turn(v, ahead):
        near, far = (quads - 1, per_tile - 1) if ahead else (1, quads - per_tile + 1)
        edge = row % per_tile == (per_tile - 1 if ahead else 0)
        return jnp.where(edge, pltpu.roll(v, far, 0), pltpu.roll(v, near, 0))

    used = [lows[1] + turn(highs[3], False), lows[2] + highs[0], lows[3] + highs[1], turn(lows[0], True) + highs[2]]
    used = jnp.maximum(jnp.maximum(used[0], used[1]), jnp.maximum(used[2], used[3]))
    line = jnp.where(jnp.max(used, axis=0, keepdims=True) > CAP, MARK, line)

    target = x.astype(F32).astype(BF)
    spot = (iota((8, 128), 1) % CAP).astype(F32)
    hole = (iota((8, 128), 0) == ELEM % 8) & (iota((8, 128), 1) // CAP == ELEM // 8)
    hole = jnp.where(hole, DEAD, 0.0)
    copies[3].wait()
    for t in range(devices // n_spec):
        msgs = []
        for a in range(t * per_tile, (t + 1) * per_tile):
            ab = abund_ref[:, a * 128 : (a + 1) * 128].astype(F32)
            vals = jnp.concatenate([ab, line[a : a + 1], pixel[a : a + 1]], axis=0).astype(BF)
            dest = jnp.broadcast_to(place[a : a + 1], (16, 128)).astype(BF)
            dest = jnp.concatenate([dest] * 8, axis=0)
            moved = nt(vals, jnp.where(dest == target, jnp.ones((), BF), jnp.zeros((), BF)))
            msgs += swap_blocks([moved[8 * j : 8 * j + 8] for j in range(4)])
        for c in range(n_spec):
            prev, after = (c - 1) % n_spec, (c + 1) % n_spec
            run = lambda v, k: v[k % 4][t * per_tile + k // 4 : t * per_tile + k // 4 + 1]
            halo = jnp.where(spot >= CAP - run(highs, prev), msgs[prev], hole)
            halo = jnp.where(spot < run(lows, after), msgs[after], halo)
            out_ref[t * n_spec + c] = jnp.concatenate([msgs[c], halo], axis=0).astype(BF)
        if (t + 1) % SENT_TILES == 0:
            part = pl.ds((t + 1 - SENT_TILES) * n_spec, SENT_TILES * n_spec)
            pltpu.make_async_copy(out_ref.at[part], out_hbm.at[part], out_sem).start()
    pltpu.make_async_copy(out_ref, out_hbm, out_sem).wait()


def prepare_kernel(doppler_ref, share_ref, table_ref, prof_ref, norm_ref, left_ref, scan_ref, tri_ref):
    offset = iota((4 * HW, 2 * HW), 1) + HW - iota((4 * HW, 2 * HW), 0)
    near = jnp.abs(offset) <= HW
    offset = offset.astype(F32)
    left_of = iota((2 * HW, 2 * HW), 1) <= iota((2 * HW, 2 * HW), 0)

    def body(i, carry):
        share = share_ref[i]
        u = offset / doppler_ref[i]
        raw = (1.0 - share) * jnp.exp(-u * u) + share / (1.0 + u * u)
        raw = jnp.where(near, raw, 0.0)
        norm_ref[i] = jnp.broadcast_to(1.0 / jnp.sum(raw, axis=0, keepdims=True), (8, 2 * HW))
        raw = jnp.where(left_of, raw[: 2 * HW], raw[2 * HW :])
        top = raw.astype(BF)
        prof_ref[i] = jnp.concatenate([top, (raw - top.astype(F32)).astype(BF)], axis=1)
        return carry

    lax.fori_loop(0, ION, body, 0)

    table = table_ref[...]
    hi = table.astype(BF)
    rest = table - hi.astype(F32)
    mid = rest.astype(BF)
    low = (rest - mid.astype(F32)).astype(BF)
    picks = jnp.where(iota((16, WIDE), 1) == iota((16, WIDE), 0) + ELEM, 1.0, 0.0)
    picks = jnp.where(iota((16, WIDE), 0) < 2, picks, 0.0).astype(BF)
    left_ref[...] = jnp.concatenate([jnp.concatenate([hi, mid, low], axis=1), picks], axis=0)

    x, y = iota((128, 128), 0), iota((128, 128), 1)
    one = lambda m: jnp.where(m, 1.0, 0.0).astype(BF)
    bucket, group, half = x // 16 == y // 16, x % 16 == y % 16, x // 64 == y // 64
    for k, m in enumerate(
        (
            bucket & (x < y),
            bucket,
            group & half & (x < y),
            group & (x < y),
            group & (x >= 64),
            group & (y < 64),
            group & (x // 64 != y // 64),
            (x % 16 == 0) & (x // 16 < y // 16),
            x % 16 == 0,
        )
    ):
        scan_ref[k] = one(m)
    tri_ref[...] = one(iota((GROUP, GROUP), 0) < iota((GROUP, GROUP), 1))


def unpack(recv_ref, rec_ref, line_ref, pixel_ref, per):
    def body(g, carry):
        tiles = [recv_ref[g * 8 + p].astype(F32) for p in range(8)]
        for kind in range(LISTS):
            halves = []
            for h in range(2):
                srcs = [tiles[4 * h + s][8 * kind : 8 * kind + 8] for s in range(4)]
                halves.append(jnp.concatenate(swap_blocks(srcs), axis=0))
            rec = jnp.concatenate(halves, axis=1)
            rec_ref[kind * per + g] = jnp.concatenate([rec.astype(BF)] * 3, axis=0)
            line_ref[pl.ds(kind * per + g, 1), :] = rec[ELEM : ELEM + 1]
            pixel_ref[pl.ds(kind * per + g, 1), :] = rec[ELEM + 1 : ELEM + 2]
        return carry

    lax.fori_loop(0, per, body, 0, unroll=4)


def rank_slots(line_ref, pixel_ref, scan_ref, tri_ref, pos_ref, info_ref, per):
    live = line_ref[...] < SL_DEV
    block = jnp.where(live, jnp.floor(pixel_ref[...] * (1.0 / PX)), -1.0)
    marks = []
    for b in range(BUCKETS):
        if b < SIDE:
            kind, which = 1, OWN - SIDE + b
        elif b < SIDE + OWN:
            kind, which = 0, b - SIDE
        else:
            kind, which = 1, b - SIDE - OWN
        marks.append(jnp.where(block[kind * per : (kind + 1) * per] == which, 1.0, 0.0).astype(BF))
    marks = jnp.concatenate(marks, axis=0)
    n = BUCKETS * per
    rank = jnp.dot(marks, tri_ref[...], preferred_element_type=F32)
    total = jnp.dot(marks, jnp.ones((GROUP, GROUP), BF), preferred_element_type=F32)
    count = nt(jnp.ones((8, GROUP), BF), marks)
    sides = [*range(SIDE), *range(SIDE + OWN, BUCKETS)]
    for kind, buckets in enumerate((range(SIDE, SIDE + OWN), sides)):
        start = jnp.zeros((per, GROUP), F32)
        place = jnp.zeros((per, GROUP), F32)
        used = jnp.zeros((per, GROUP), F32)
        for b in buckets:
            rows = slice(b * per, (b + 1) * per)
            mark = marks[rows].astype(F32)
            place = place + mark * (start + rank[rows])
            used = used + mark
            start = start + total[rows]
        pos_ref[kind * per : (kind + 1) * per] = jnp.where(used > 0, place, NOWHERE)
    times = lambda a, k: jnp.dot(a, scan_ref[k], preferred_element_type=F32)
    join = lambda a: jnp.concatenate(a, axis=1)
    c = [count[:, 128 * k : 128 * k + 128].astype(BF) for k in range(3)]
    ahead, whole = (join([times(a, k) for a in c]) for k in (0, 1))
    source = join(
        [
            times(c[0], 2),
            times(c[1], 3) + times(c[0], 4),
            times(c[2], 2) + times(c[1], 5) + times(c[0], 6),
        ]
    )
    supers = jnp.maximum(jnp.floor((whole + (SUPER - 1)) * (1.0 / SUPER)), 1.0)
    d = [supers[:, 128 * k : 128 * k + 128].astype(BF) for k in range(3)]
    first = join(
        [
            times(d[0], 7),
            times(d[1], 7) + times(d[0], 8),
            times(d[2], 7) + times(d[1], 8) + times(d[0], 8),
        ]
    )
    lane = iota((8, n), 1)
    b = lane // per
    kind = jnp.where((b >= SIDE) & (b < SIDE + OWN), 0, 1)
    base = ((kind * per + lane % per) * PITCH).astype(F32)
    longest = jnp.broadcast_to(jnp.max(count, axis=1, keepdims=True), (8, n))
    row = iota((8, n), 0)
    info = jnp.zeros((8, n), F32)
    marked = jnp.max(jnp.max(line_ref[...], axis=1, keepdims=True), axis=0, keepdims=True)
    marked = jnp.broadcast_to(marked, (8, n))
    values = (source + base, first * SUPER + ahead, count, first, whole, supers, longest, marked)
    for k, value in enumerate(values):
        info = jnp.where(row == k, value, info)
    info_ref[...] = info.astype(I32)


def sort_groups(rec_ref, pos_ref, sorted_ref, groups):
    target = iota((GROUP, GROUP), 0).astype(F32).astype(BF)

    def body(g, carry):
        pos = jnp.broadcast_to(pos_ref[pl.ds(g, 1), :], (16, GROUP)).astype(BF)
        pos = jnp.concatenate([pos] * (GROUP // 16), axis=0)
        perm = jnp.where(pos == target, jnp.ones((), BF), jnp.zeros((), BF))
        sorted_ref[pl.ds(pl.multiple_of(g * PITCH, 8), GROUP), :] = nt(perm, rec_ref[g])
        return carry

    lax.fori_loop(0, groups, body, 0, unroll=32)


def join_runs(info, sorted_ref, rows_ref, n):
    def body(k, carry):
        rows_ref[pl.ds(info[1, k], STEP), :] = sorted_ref[pl.ds(info[0, k], STEP), :]
        return carry

    lax.fori_loop(0, n, body, 0, unroll=32)

    @pl.when(info[6, 0] > STEP)
    def _():
        def tail(k, carry):
            def one(r, c):
                rows_ref[pl.ds(info[1, k] + r, 1), :] = sorted_ref[pl.ds(info[0, k] + r, 1), :]
                return c

            lax.fori_loop(STEP, info[2, k], one, 0)
            return carry

        lax.fori_loop(0, n, tail, 0)


def make_columns(info, left_ref, rows_ref, cols_ref, per):
    def body(k, carry):
        at = pl.multiple_of(k * (BATCH * SUPER), BATCH * SUPER)
        got = nt(left_ref[...], rows_ref[pl.ds(at, BATCH * SUPER), :].astype(BF))
        for m in range(BATCH):
            cols_ref[k * BATCH + m] = got[:, m * SUPER : (m + 1) * SUPER]
        return carry

    lax.fori_loop(0, BUCKETS // BATCH, body, 0, unroll=6)
    last = (BUCKETS - 1) * per
    lax.fori_loop(BUCKETS // BATCH, (info[3, last] + info[5, last] + BATCH - 1) // BATCH, body, 0)


def deposit(info, cols_ref, grid_ref, low_ref, acc_ref, energy_ref, per):
    lane = iota((1, SUPER), 1)
    pixels = iota((PX, SUPER), 0).astype(F32).astype(BF)
    lines = iota((SL_DEV, SUPER), 0).astype(F32).astype(BF)
    one, zero = jnp.ones((), BF), jnp.zeros((), BF)
    last = (BUCKETS - 1) * per
    crowded = info[3, last] + info[5, last] > BUCKETS

    def packed(row):
        return jnp.broadcast_to(row, (16, SUPER)).astype(BF)

    def product(s, count):
        pixel = cols_ref[s, ION + 1 : ION + 2, :]
        pixel = jnp.where(lane < count, pixel - PX * jnp.floor(pixel * (1.0 / PX)), NOWHERE)
        here = packed(pixel) == pixels
        cols = cols_ref[s, :ION, :]
        size = jnp.sqrt(jnp.sum(cols * cols, axis=0, keepdims=True))
        spread = [jnp.where(here, packed(cols_ref[s, i : i + 1, :]), zero) for i in range(ION)]
        spread += [jnp.where(here, packed(size), zero), jnp.where(here, one, zero)]
        line = jnp.concatenate([packed(cols_ref[s, ION : ION + 1, :])] * (SL_DEV // 16), axis=0)
        return nt(jnp.concatenate(spread, axis=0), jnp.where(line == lines, one, zero))

    def place(b):
        return pl.ds(pl.multiple_of(b * PX, PX), PX)

    energy_ref[...] = jnp.zeros_like(energy_ref)

    def body(b, carry):
        value = product(info[3, b * per], info[4, b * per])
        for i in range(ION):
            grid_ref[i, place(b), :] = value[i * PX : (i + 1) * PX].astype(BF)
        energy = value[ION * PX : (ION + 1) * PX]
        energy = energy * energy
        energy_ref[0] += energy
        energy_ref[1] += jnp.where(value[(ION + 1) * PX :] > 1.5, energy, 0.0)
        return carry

    lax.fori_loop(0, BUCKETS, body, 0, unroll=24)
    fine = crowded | (jnp.sum(energy_ref[1]) > SHARED * jnp.sum(energy_ref[0]))

    @pl.when(fine)
    def _():
        def again(b, carry):
            k = b * per
            acc_ref[...] = jnp.zeros_like(acc_ref)

            def more(s, c):
                acc_ref[...] += product(info[3, k] + s, info[4, k] - s * SUPER)
                return c

            lax.fori_loop(0, info[5, k], more, 0)
            for i in range(ION):
                value = acc_ref[i * PX : (i + 1) * PX, :]
                top = value.astype(BF)
                grid_ref[i, place(b), :] = top
                low_ref[i, place(b), :] = (value - top.astype(F32)).astype(BF)
            return carry

        lax.fori_loop(0, BUCKETS, again, 0)

    return fine


def broaden(grid_ref, low_ref, fine, prof_ref, norm_ref, out_hbm, out_ref, sem):
    row, col = iota((2 * HW, 4 * HW), 0), iota((2 * HW, 4 * HW), 1) % (2 * HW)
    zero = jnp.zeros((), F32)
    upper, lower = (jnp.where(m, 1.0, zero).astype(BF) > jnp.zeros((), BF) for m in (col <= row, col >= row))

    def halves(planes, i, at):
        shape = prof_ref[i]
        shape = jnp.concatenate([jnp.where(m, shape, jnp.zeros((), BF)) for m in (upper, lower)], axis=0)
        both = sum(tn(p[at : at + 4 * HW], shape) for p in planes)
        return (both[:, : 2 * HW] + both[:, 2 * HW :]) * norm_ref[i, 0:1]

    def run(refs, unroll):
        def body(q, carry):
            for j in range(unroll):
                i = q * unroll + j
                planes = [ref[i] for ref in refs]
                out_ref[i, :, :128] = halves(planes, i, 0)
                out_ref[i, :, 128:] = halves(planes, i, 2 * HW)
                pltpu.make_async_copy(out_ref.at[i], out_hbm.at[i], sem).start()
            return carry

        lax.fori_loop(0, ION // unroll, body, 0)

    @pl.when(fine)
    def _():
        run((grid_ref, low_ref), 1)

    @pl.when(jnp.logical_not(fine))
    def _():
        run((grid_ref,), QUAD)

    pltpu.make_async_copy(out_ref, out_hbm, sem).wait()


def main_kernel(recv_ref, left_ref, norm_ref, scan_ref, tri_ref, prof_ref, out_hbm, again_ref, rec_ref, line_ref, pixel_ref,
                pos_ref, info_ref, sorted_ref, rows_ref, cols_ref, grid_ref, low_ref, acc_ref, energy_ref, out_ref, info, sem,
                out_sem):
    groups = rec_ref.shape[0]
    per = groups // LISTS
    unpack(recv_ref, rec_ref, line_ref, pixel_ref, per)
    rank_slots(line_ref, pixel_ref, scan_ref, tri_ref, pos_ref, info_ref, per)
    to_scalars = pltpu.make_async_copy(info_ref, info, sem)
    to_scalars.start()
    sort_groups(rec_ref, pos_ref, sorted_ref, groups)
    to_scalars.wait()
    again_ref[0] = jnp.where(info[7, 0] >= MARK, 1, 0)
    join_runs(info, sorted_ref, rows_ref, BUCKETS * per)
    make_columns(info, left_ref, rows_ref, cols_ref, per)
    fine = deposit(info, cols_ref, grid_ref, low_ref, acc_ref, energy_ref, per)
    broaden(grid_ref, low_ref, fine, prof_ref, norm_ref, out_hbm, out_ref, out_sem)


def direct(abundances, sightline, pixel, counts, ion_table, doppler, lorentz_share):
    n_spec = lax.axis_size("spec")
    devices = lax.axis_size("los") * n_spec
    n_slots = abundances.shape[1]
    vmem = pl.BlockSpec(memory_space=pltpu.VMEM)
    smem = pl.BlockSpec(memory_space=pltpu.SMEM)
    anywhere = pl.BlockSpec(memory_space=pltpu.HBM)
    sent = pl.pallas_call(
        lambda *refs: pack_kernel(*refs, n_spec=n_spec),
        out_shape=jax.ShapeDtypeStruct((devices, LISTS * 8, 128), BF),
        in_specs=[anywhere] * 4,
        out_specs=anywhere,
        scratch_shapes=[
            pltpu.VMEM(abundances.shape, BF),
            pltpu.VMEM((n_slots // 128, 128), I32),
            pltpu.VMEM((n_slots // 128, 128), I32),
            pltpu.VMEM(counts.shape, I32),
            pltpu.VMEM((devices, LISTS * 8, 128), BF),
            pltpu.SemaphoreType.DMA((4,)),
            pltpu.SemaphoreType.DMA,
        ],
        compiler_params=pltpu.CompilerParams(vmem_limit_bytes=63 * 2**20),
        name="pack",
    )(abundances, sightline.reshape(n_slots // 128, 128), pixel.reshape(n_slots // 128, 128), counts)
    groups = LISTS * n_slots // GROUP
    n = BUCKETS * groups // LISTS
    table = jnp.pad(ion_table.T, ((0, 0), (0, VAL - ELEM)))
    prof, norm, left, scan, tri = pl.pallas_call(
        prepare_kernel,
        out_shape=[
            jax.ShapeDtypeStruct((ION, 2 * HW, 4 * HW), BF),
            jax.ShapeDtypeStruct((ION, 8, 2 * HW), F32),
            jax.ShapeDtypeStruct((OUTS, WIDE), BF),
            jax.ShapeDtypeStruct((9, 128, 128), BF),
            jax.ShapeDtypeStruct((GROUP, GROUP), BF),
        ],
        in_specs=[smem, smem, vmem],
        out_specs=[vmem] * 5,
        compiler_params=pltpu.CompilerParams(vmem_limit_bytes=10 * 2**20),
        cost_estimate=pl.CostEstimate(flops=20_000_000, bytes_accessed=4 * 2**20, transcendentals=3_000_000),
        name="prepare",
    )(doppler, lorentz_share, table)
    got = lax.all_to_all(sent, ("los", "spec"), split_axis=0, concat_axis=0, tiled=True)
    supers = LISTS * n_slots // SUPER + BUCKETS
    return pl.pallas_call(
        main_kernel,
        out_shape=[jax.ShapeDtypeStruct((ION, SL_DEV, PIX_DEV), F32), jax.ShapeDtypeStruct((1,), I32)],
        in_specs=[vmem] * 6,
        out_specs=[anywhere, smem],
        scratch_shapes=[
            pltpu.VMEM((groups, WIDE, GROUP), BF),
            pltpu.VMEM((groups, GROUP), F32),
            pltpu.VMEM((groups, GROUP), F32),
            pltpu.VMEM((groups, GROUP), F32),
            pltpu.VMEM((8, n), I32),
            pltpu.VMEM((groups * PITCH, WIDE), F32),
            pltpu.VMEM((supers * SUPER + STEP, WIDE), F32),
            pltpu.VMEM((supers, OUTS, SUPER), F32),
            pltpu.VMEM((ION, BUCKETS * PX, SL_DEV), BF),
            pltpu.VMEM((ION, BUCKETS * PX, SL_DEV), BF),
            pltpu.VMEM(((ION + 2) * PX, SL_DEV), F32),
            pltpu.VMEM((2, PX, SL_DEV), F32),
            pltpu.VMEM((ION, SL_DEV, PIX_DEV), F32),
            pltpu.SMEM((8, n), I32),
            pltpu.SemaphoreType.DMA,
            pltpu.SemaphoreType.DMA,
        ],
        compiler_params=pltpu.CompilerParams(vmem_limit_bytes=41 * 2**20),
        name="deposit_broaden",
    )(got, left, norm, scan, tri, prof)


def with_halo(cells, sides, width):
    for axis, dim in sides:
        count = lax.axis_size(axis)
        head = lax.slice_in_dim(cells, 0, width, axis=dim)
        tail = lax.slice_in_dim(cells, cells.shape[dim] - width, cells.shape[dim], axis=dim)
        cells = jnp.concatenate(
            [
                lax.ppermute(tail, axis, [(i, (i + 1) % count) for i in range(count)]),
                cells,
                lax.ppermute(head, axis, [((i + 1) % count, i) for i in range(count)]),
            ],
            axis=dim,
        )
    return cells


def line_shape(offset, doppler, share):
    u = offset / doppler
    return (1.0 - share) * jnp.exp(-u * u) + share / (1.0 + u * u)


def deposit_onto(got_cols, line_rows, place, span):
    ions = got_cols.shape[0]
    n_rows = got_cols.shape[1]
    pixel_hot = (place[:, None] == lax.broadcasted_iota(jnp.int32, (1, span), 1)).astype(
        jnp.bfloat16
    )
    line_hot = (line_rows[None, :] == lax.broadcasted_iota(jnp.int32, (SL_DEV, 1), 0)).astype(
        jnp.bfloat16
    )
    group = 8
    grouped = got_cols.reshape(ions // group, group, n_rows)

    def deposit(part_cols):
        spread = (part_cols[:, None, :] * line_hot[None, :, :]).reshape(group * SL_DEV, n_rows)
        return jnp.dot(spread, pixel_hot, preferred_element_type=jnp.float32).reshape(
            group, SL_DEV, span
        )

    return lax.map(deposit, grouped).reshape(ions, SL_DEV, span)


def broaden_window(padded, pix_dev, width, share, norm):
    inner = lax.broadcasted_iota(jnp.int32, (pix_dev + 2 * HW, pix_dev), 0)
    outer = lax.broadcasted_iota(jnp.int32, (pix_dev + 2 * HW, pix_dev), 1)
    delta = (outer + HW - inner).astype(jnp.float32)[None, :, :]
    matrix = jnp.where(jnp.abs(delta) <= HW, line_shape(delta, width, share), 0.0) / norm
    return jnp.einsum("isk,ikj->isj", padded, matrix, precision=lax.Precision.HIGHEST)


def general(abundances, sightline, pixel, counts, ion_table, doppler, lorentz_share):
    n_los = lax.axis_size("los")
    n_spec = lax.axis_size("spec")
    devices = n_los * n_spec
    n_slots = abundances.shape[1]
    slots = n_slots // devices
    pix_dev = PIXELS // n_spec
    columns = jnp.dot(ion_table.T, abundances.astype(jnp.float32), precision=lax.Precision.HIGHEST)
    live = lax.broadcasted_iota(jnp.int32, (devices, slots), 1) < counts[0][:, None]
    columns = jnp.where(live.reshape(1, n_slots), columns, 0.0).astype(jnp.bfloat16)
    cell = (sightline * pix_dev + pixel).reshape(1, n_slots)
    got_cols, got_cell = (
        lax.all_to_all(columns, ("los", "spec"), split_axis=1, concat_axis=1, tiled=True),
        lax.all_to_all(cell, ("los", "spec"), split_axis=1, concat_axis=1, tiled=True),
    )
    got_cell = got_cell.reshape(n_slots)
    grid = deposit_onto(got_cols, got_cell // pix_dev, got_cell % pix_dev, pix_dev)
    offsets = jnp.arange(-HW, HW + 1).astype(jnp.float32)
    totals = jnp.sum(line_shape(offsets[None, :], doppler[:, None], lorentz_share[:, None]), axis=1)
    width = doppler[:, None, None]
    share = lorentz_share[:, None, None]
    norm = totals[:, None, None]
    padded = with_halo(grid, (("spec", 2),), HW)
    depth = broaden_window(padded, pix_dev, width, share, norm)
    return depth


def on_device(*args):
    depth, again = direct(*args)
    return lax.fori_loop(0, again[0], lambda _, old: general(*args), depth)


def solution(mesh):
    in_specs = (
        P(None, ("los", "spec")),
        P(("los", "spec")),
        P(("los", "spec")),
        P(("los", "spec"), None),
        P(),
        P(),
        P(),
    )
    return jax.shard_map(
        on_device, mesh=mesh, in_specs=in_specs, out_specs=P(None, "los", "spec"), check_vma=False
    )
```

```python
import jax
import jax.numpy as jnp
from jax import lax
from jax.experimental import pallas as pl
from jax.experimental.pallas import tpu as pltpu
from jax.sharding import PartitionSpec as P

ELEM = 30
ION = 32
VAL = 32
WIDE = 3 * VAL
OUTS = ION + 16
BATCH = 4
HW = 64
SL_DEV = 256
PIX_DEV = 256
PIXELS = 4096
CAP = 32
DEAD = 256.0
MARK = 384.0
NOWHERE = 512.0
LISTS = 2
GROUP = 256
SUPER = 256
PX = 16
SIDE = HW // PX
OWN = PIX_DEV // PX
BUCKETS = OWN + 2 * SIDE
SHARED = 0.15
QUAD = 32
STEP = 32
PITCH = GROUP + STEP
SENT_TILES = 2
BF = jnp.bfloat16
F32 = jnp.float32
I32 = jnp.int32


def iota(shape, dim):
    return lax.broadcasted_iota(I32, shape, dim)


def nt(a, b):
    return lax.dot_general(a, b, (((1,), (1,)), ((), ())), preferred_element_type=F32)


def tn(a, b):
    return lax.dot_general(a, b, (((0,), (0,)), ((), ())), preferred_element_type=F32)


def swap_blocks(tiles):
    lane = iota((8, 128), 1)
    low = lane < 64
    even = (lane // 32) % 2 == 0
    far = [pltpu.roll(t, 64, 1) for t in tiles]
    half = [
        jnp.where(low, tiles[0], far[2]),
        jnp.where(low, tiles[1], far[3]),
        jnp.where(low, far[0], tiles[2]),
        jnp.where(low, far[1], tiles[3]),
    ]
    out = [None] * 4
    for p in (0, 2):
        a, b = half[p], half[p + 1]
        out[p] = jnp.where(even, a, pltpu.roll(b, 32, 1))
        out[p + 1] = jnp.where(even, pltpu.roll(a, 96, 1), b)
    return out


def pack_kernel(abund_hbm, line_hbm, pixel_hbm, counts_hbm, out_hbm, abund_ref, line_ref, pixel_ref, counts_ref,
                out_ref, sems, out_sem, *, n_spec):
    copies = [
        pltpu.make_async_copy(src, dst, sems.at[k])
        for k, (src, dst) in enumerate(
            ((counts_hbm, counts_ref), (line_hbm, line_ref), (pixel_hbm, pixel_ref), (abund_hbm, abund_ref))
        )
    ]
    for copy in copies:
        copy.start()
    devices = counts_ref.shape[1]
    quads = devices // 4
    per_tile = n_spec // 4
    one = lambda m: jnp.where(m, 1.0, 0.0).astype(BF)
    dot = lambda a, b: jnp.dot(a, b, preferred_element_type=F32)
    x, y = iota((128, 128), 0), iota((128, 128), 1)
    same = x // CAP == y // CAP
    lane = iota((quads, 128), 1)
    row = iota((quads, 128), 0)
    slot = (lane % CAP).astype(F32)
    pick = one(iota((devices, 128), 0) % 4 == iota((devices, 128), 1) // CAP)
    for copy in copies[:3]:
        copy.wait()
    owner = iota((quads, devices), 1) // 4 == iota((quads, devices), 0)
    live = slot < dot(jnp.where(owner, counts_ref[...].astype(F32), 0.0).astype(BF), pick)
    line = jnp.where(live, line_ref[...].astype(F32), DEAD)
    pixel = pixel_ref[...].astype(F32)

    low = jnp.where(live & (pixel < HW), 1.0, 0.0)
    high = jnp.where(live & (pixel >= PIX_DEV - HW), 1.0, 0.0)
    marks = jnp.concatenate([low, 1.0 - low - high, high], axis=0).astype(BF)
    rank = dot(marks, one(same & (x < y)))
    total = dot(marks, one(same))
    n_low, n_high = total[:quads], total[2 * quads :]
    place = jnp.where(high > 0, CAP - n_high + rank[2 * quads :], n_low + rank[quads : 2 * quads])
    place = jnp.where(low > 0, rank[:quads], place) + (lane // CAP * CAP).astype(F32)
    ends = jnp.concatenate([n_low, n_high], axis=0).astype(BF)
    ends = [dot(ends, one(x == CAP * b)) for b in range(4)]
    lows = [e[:quads] for e in ends]
    highs = [e[quads:] for e in ends]

    def turn(v, ahead):
        near, far = (quads - 1, per_tile - 1) if ahead else (1, quads - per_tile + 1)
        edge = row % per_tile == (per_tile - 1 if ahead else 0)
        return jnp.where(edge, pltpu.roll(v, far, 0), pltpu.roll(v, near, 0))

    used = [lows[1] + turn(highs[3], False), lows[2] + highs[0], lows[3] + highs[1], turn(lows[0], True) + highs[2]]
    used = jnp.maximum(jnp.maximum(used[0], used[1]), jnp.maximum(used[2], used[3]))
    line = jnp.where(jnp.max(used, axis=0, keepdims=True) > CAP, MARK, line)

    target = x.astype(F32).astype(BF)
    spot = (iota((8, 128), 1) % CAP).astype(F32)
    hole = (iota((8, 128), 0) == ELEM % 8) & (iota((8, 128), 1) // CAP == ELEM // 8)
    hole = jnp.where(hole, DEAD, 0.0)
    copies[3].wait()
    for t in range(devices // n_spec):
        msgs = []
        for a in range(t * per_tile, (t + 1) * per_tile):
            ab = abund_ref[:, a * 128 : (a + 1) * 128].astype(F32)
            vals = jnp.concatenate([ab, line[a : a + 1], pixel[a : a + 1]], axis=0).astype(BF)
            dest = jnp.broadcast_to(place[a : a + 1], (16, 128)).astype(BF)
            dest = jnp.concatenate([dest] * 8, axis=0)
            moved = nt(vals, jnp.where(dest == target, jnp.ones((), BF), jnp.zeros((), BF)))
            msgs += swap_blocks([moved[8 * j : 8 * j + 8] for j in range(4)])
        for c in range(n_spec):
            prev, after = (c - 1) % n_spec, (c + 1) % n_spec
            run = lambda v, k: v[k % 4][t * per_tile + k // 4 : t * per_tile + k // 4 + 1]
            halo = jnp.where(spot >= CAP - run(highs, prev), msgs[prev], hole)
            halo = jnp.where(spot < run(lows, after), msgs[after], halo)
            out_ref[t * n_spec + c] = jnp.concatenate([msgs[c], halo], axis=0).astype(BF)
        if (t + 1) % SENT_TILES == 0:
            part = pl.ds((t + 1 - SENT_TILES) * n_spec, SENT_TILES * n_spec)
            pltpu.make_async_copy(out_ref.at[part], out_hbm.at[part], out_sem).start()
    pltpu.make_async_copy(out_ref, out_hbm, out_sem).wait()


def prepare_kernel(doppler_ref, share_ref, table_ref, prof_ref, norm_ref, left_ref, scan_ref, tri_ref):
    offset = iota((4 * HW, 2 * HW), 1) + HW - iota((4 * HW, 2 * HW), 0)
    near = jnp.abs(offset) <= HW
    offset = offset.astype(F32)
    left_of = iota((2 * HW, 2 * HW), 1) <= iota((2 * HW, 2 * HW), 0)

    def body(i, carry):
        share = share_ref[i]
        u = offset / doppler_ref[i]
        raw = (1.0 - share) * jnp.exp(-u * u) + share / (1.0 + u * u)
        raw = jnp.where(near, raw, 0.0)
        norm_ref[i] = jnp.broadcast_to(1.0 / jnp.sum(raw, axis=0, keepdims=True), (8, 2 * HW))
        raw = jnp.where(left_of, raw[: 2 * HW], raw[2 * HW :])
        top = raw.astype(BF)
        prof_ref[i] = jnp.concatenate([top, (raw - top.astype(F32)).astype(BF)], axis=1)
        return carry

    lax.fori_loop(0, ION, body, 0)

    table = table_ref[...]
    hi = table.astype(BF)
    rest = table - hi.astype(F32)
    mid = rest.astype(BF)
    low = (rest - mid.astype(F32)).astype(BF)
    picks = jnp.where(iota((16, WIDE), 1) == iota((16, WIDE), 0) + ELEM, 1.0, 0.0)
    picks = jnp.where(iota((16, WIDE), 0) < 2, picks, 0.0).astype(BF)
    left_ref[...] = jnp.concatenate([jnp.concatenate([hi, mid, low], axis=1), picks], axis=0)

    x, y = iota((128, 128), 0), iota((128, 128), 1)
    one = lambda m: jnp.where(m, 1.0, 0.0).astype(BF)
    bucket, group, half = x // 16 == y // 16, x % 16 == y % 16, x // 64 == y // 64
    for k, m in enumerate(
        (
            bucket & (x < y),
            bucket,
            group & half & (x < y),
            group & (x < y),
            group & (x >= 64),
            group & (y < 64),
            group & (x // 64 != y // 64),
            (x % 16 == 0) & (x // 16 < y // 16),
            x % 16 == 0,
        )
    ):
        scan_ref[k] = one(m)
    tri_ref[...] = one(iota((GROUP, GROUP), 0) < iota((GROUP, GROUP), 1))


def unpack(recv_ref, rec_ref, line_ref, pixel_ref, per):
    def body(g, carry):
        tiles = [recv_ref[g * 8 + p].astype(F32) for p in range(8)]
        for kind in range(LISTS):
            halves = []
            for h in range(2):
                srcs = [tiles[4 * h + s][8 * kind : 8 * kind + 8] for s in range(4)]
                halves.append(jnp.concatenate(swap_blocks(srcs), axis=0))
            rec = jnp.concatenate(halves, axis=1)
            rec_ref[kind * per + g] = jnp.concatenate([rec.astype(BF)] * 3, axis=0)
            line_ref[pl.ds(kind * per + g, 1), :] = rec[ELEM : ELEM + 1]
            pixel_ref[pl.ds(kind * per + g, 1), :] = rec[ELEM + 1 : ELEM + 2]
        return carry

    lax.fori_loop(0, per, body, 0, unroll=4)


def rank_slots(line_ref, pixel_ref, scan_ref, tri_ref, pos_ref, info_ref, per):
    live = line_ref[...] < SL_DEV
    block = jnp.where(live, jnp.floor(pixel_ref[...] * (1.0 / PX)), -1.0)
    marks = []
    for b in range(BUCKETS):
        if b < SIDE:
            kind, which = 1, OWN - SIDE + b
        elif b < SIDE + OWN:
            kind, which = 0, b - SIDE
        else:
            kind, which = 1, b - SIDE - OWN
        marks.append(jnp.where(block[kind * per : (kind + 1) * per] == which, 1.0, 0.0).astype(BF))
    marks = jnp.concatenate(marks, axis=0)
    n = BUCKETS * per
    rank = jnp.dot(marks, tri_ref[...], preferred_element_type=F32)
    total = jnp.dot(marks, jnp.ones((GROUP, GROUP), BF), preferred_element_type=F32)
    count = nt(jnp.ones((8, GROUP), BF), marks)
    sides = [*range(SIDE), *range(SIDE + OWN, BUCKETS)]
    for kind, buckets in enumerate((range(SIDE, SIDE + OWN), sides)):
        start = jnp.zeros((per, GROUP), F32)
        place = jnp.zeros((per, GROUP), F32)
        used = jnp.zeros((per, GROUP), F32)
        for b in buckets:
            rows = slice(b * per, (b + 1) * per)
            mark = marks[rows].astype(F32)
            place = place + mark * (start + rank[rows])
            used = used + mark
            start = start + total[rows]
        pos_ref[kind * per : (kind + 1) * per] = jnp.where(used > 0, place, NOWHERE)
    times = lambda a, k: jnp.dot(a, scan_ref[k], preferred_element_type=F32)
    join = lambda a: jnp.concatenate(a, axis=1)
    c = [count[:, 128 * k : 128 * k + 128].astype(BF) for k in range(3)]
    ahead, whole = (join([times(a, k) for a in c]) for k in (0, 1))
    source = join(
        [
            times(c[0], 2),
            times(c[1], 3) + times(c[0], 4),
            times(c[2], 2) + times(c[1], 5) + times(c[0], 6),
        ]
    )
    supers = jnp.maximum(jnp.floor((whole + (SUPER - 1)) * (1.0 / SUPER)), 1.0)
    d = [supers[:, 128 * k : 128 * k + 128].astype(BF) for k in range(3)]
    first = join(
        [
            times(d[0], 7),
            times(d[1], 7) + times(d[0], 8),
            times(d[2], 7) + times(d[1], 8) + times(d[0], 8),
        ]
    )
    lane = iota((8, n), 1)
    b = lane // per
    kind = jnp.where((b >= SIDE) & (b < SIDE + OWN), 0, 1)
    base = ((kind * per + lane % per) * PITCH).astype(F32)
    longest = jnp.broadcast_to(jnp.max(count, axis=1, keepdims=True), (8, n))
    row = iota((8, n), 0)
    info = jnp.zeros((8, n), F32)
    marked = jnp.max(jnp.max(line_ref[...], axis=1, keepdims=True), axis=0, keepdims=True)
    marked = jnp.broadcast_to(marked, (8, n))
    values = (source + base, first * SUPER + ahead, count, first, whole, supers, longest, marked)
    for k, value in enumerate(values):
        info = jnp.where(row == k, value, info)
    info_ref[...] = info.astype(I32)


def sort_groups(rec_ref, pos_ref, sorted_ref, groups):
    target = iota((GROUP, GROUP), 0).astype(F32).astype(BF)

    def body(g, carry):
        pos = jnp.broadcast_to(pos_ref[pl.ds(g, 1), :], (16, GROUP)).astype(BF)
        pos = jnp.concatenate([pos] * (GROUP // 16), axis=0)
        perm = jnp.where(pos == target, jnp.ones((), BF), jnp.zeros((), BF))
        sorted_ref[pl.ds(pl.multiple_of(g * PITCH, 8), GROUP), :] = nt(perm, rec_ref[g])
        return carry

    lax.fori_loop(0, groups, body, 0, unroll=32)


def join_runs(info, sorted_ref, rows_ref, n):
    def body(k, carry):
        rows_ref[pl.ds(info[1, k], STEP), :] = sorted_ref[pl.ds(info[0, k], STEP), :]
        return carry

    lax.fori_loop(0, n, body, 0, unroll=32)

    @pl.when(info[6, 0] > STEP)
    def _():
        def tail(k, carry):
            def one(r, c):
                rows_ref[pl.ds(info[1, k] + r, 1), :] = sorted_ref[pl.ds(info[0, k] + r, 1), :]
                return c

            lax.fori_loop(STEP, info[2, k], one, 0)
            return carry

        lax.fori_loop(0, n, tail, 0)


def make_columns(info, left_ref, rows_ref, cols_ref, per):
    def body(k, carry):
        at = pl.multiple_of(k * (BATCH * SUPER), BATCH * SUPER)
        got = nt(left_ref[...], rows_ref[pl.ds(at, BATCH * SUPER), :].astype(BF))
        for m in range(BATCH):
            cols_ref[k * BATCH + m] = got[:, m * SUPER : (m + 1) * SUPER]
        return carry

    lax.fori_loop(0, BUCKETS // BATCH, body, 0, unroll=6)
    last = (BUCKETS - 1) * per
    lax.fori_loop(BUCKETS // BATCH, (info[3, last] + info[5, last] + BATCH - 1) // BATCH, body, 0)


def deposit(info, cols_ref, grid_ref, low_ref, acc_ref, energy_ref, per):
    lane = iota((1, SUPER), 1)
    pixels = iota((PX, SUPER), 0).astype(F32).astype(BF)
    lines = iota((SL_DEV, SUPER), 0).astype(F32).astype(BF)
    one, zero = jnp.ones((), BF), jnp.zeros((), BF)
    last = (BUCKETS - 1) * per
    crowded = info[3, last] + info[5, last] > BUCKETS

    def packed(row):
        return jnp.broadcast_to(row, (16, SUPER)).astype(BF)

    def product(s, count):
        pixel = cols_ref[s, ION + 1 : ION + 2, :]
        pixel = jnp.where(lane < count, pixel - PX * jnp.floor(pixel * (1.0 / PX)), NOWHERE)
        here = packed(pixel) == pixels
        cols = cols_ref[s, :ION, :]
        size = jnp.sqrt(jnp.sum(cols * cols, axis=0, keepdims=True))
        spread = [jnp.where(here, packed(cols_ref[s, i : i + 1, :]), zero) for i in range(ION)]
        spread += [jnp.where(here, packed(size), zero), jnp.where(here, one, zero)]
        line = jnp.concatenate([packed(cols_ref[s, ION : ION + 1, :])] * (SL_DEV // 16), axis=0)
        return nt(jnp.concatenate(spread, axis=0), jnp.where(line == lines, one, zero))

    def place(b):
        return pl.ds(pl.multiple_of(b * PX, PX), PX)

    energy_ref[...] = jnp.zeros_like(energy_ref)

    def body(b, carry):
        value = product(info[3, b * per], info[4, b * per])
        for i in range(ION):
            grid_ref[i, place(b), :] = value[i * PX : (i + 1) * PX].astype(BF)
        energy = value[ION * PX : (ION + 1) * PX]
        energy = energy * energy
        energy_ref[0] += energy
        energy_ref[1] += jnp.where(value[(ION + 1) * PX :] > 1.5, energy, 0.0)
        return carry

    lax.fori_loop(0, BUCKETS, body, 0, unroll=24)
    fine = crowded | (jnp.sum(energy_ref[1]) > SHARED * jnp.sum(energy_ref[0]))

    @pl.when(fine)
    def _():
        def again(b, carry):
            k = b * per
            acc_ref[...] = jnp.zeros_like(acc_ref)

            def more(s, c):
                acc_ref[...] += product(info[3, k] + s, info[4, k] - s * SUPER)
                return c

            lax.fori_loop(0, info[5, k], more, 0)
            for i in range(ION):
                value = acc_ref[i * PX : (i + 1) * PX, :]
                top = value.astype(BF)
                grid_ref[i, place(b), :] = top
                low_ref[i, place(b), :] = (value - top.astype(F32)).astype(BF)
            return carry

        lax.fori_loop(0, BUCKETS, again, 0)

    return fine


def broaden(grid_ref, low_ref, fine, prof_ref, norm_ref, out_hbm, out_ref, sem):
    row, col = iota((2 * HW, 4 * HW), 0), iota((2 * HW, 4 * HW), 1) % (2 * HW)
    zero = jnp.zeros((), F32)
    upper, lower = (jnp.where(m, 1.0, zero).astype(BF) > jnp.zeros((), BF) for m in (col <= row, col >= row))

    def halves(planes, i, at):
        shape = prof_ref[i]
        shape = jnp.concatenate([jnp.where(m, shape, jnp.zeros((), BF)) for m in (upper, lower)], axis=0)
        both = sum(tn(p[at : at + 4 * HW], shape) for p in planes)
        return (both[:, : 2 * HW] + both[:, 2 * HW :]) * norm_ref[i, 0:1]

    def run(refs, unroll):
        def body(q, carry):
            for j in range(unroll):
                i = q * unroll + j
                planes = [ref[i] for ref in refs]
                out_ref[i, :, :128] = halves(planes, i, 0)
                out_ref[i, :, 128:] = halves(planes, i, 2 * HW)
                pltpu.make_async_copy(out_ref.at[i], out_hbm.at[i], sem).start()
            return carry

        lax.fori_loop(0, ION // unroll, body, 0)

    @pl.when(fine)
    def _():
        run((grid_ref, low_ref), 1)

    @pl.when(jnp.logical_not(fine))
    def _():
        run((grid_ref,), QUAD)

    pltpu.make_async_copy(out_ref, out_hbm, sem).wait()


def main_kernel(recv_ref, left_ref, norm_ref, scan_ref, tri_ref, prof_ref, out_hbm, again_ref, rec_ref, line_ref, pixel_ref,
                pos_ref, info_ref, sorted_ref, rows_ref, cols_ref, grid_ref, low_ref, acc_ref, energy_ref, out_ref, info, sem,
                out_sem):
    groups = rec_ref.shape[0]
    per = groups // LISTS
    unpack(recv_ref, rec_ref, line_ref, pixel_ref, per)
    rank_slots(line_ref, pixel_ref, scan_ref, tri_ref, pos_ref, info_ref, per)
    to_scalars = pltpu.make_async_copy(info_ref, info, sem)
    to_scalars.start()
    sort_groups(rec_ref, pos_ref, sorted_ref, groups)
    to_scalars.wait()
    again_ref[0] = jnp.where(info[7, 0] >= MARK, 1, 0)
    join_runs(info, sorted_ref, rows_ref, BUCKETS * per)
    make_columns(info, left_ref, rows_ref, cols_ref, per)
    fine = deposit(info, cols_ref, grid_ref, low_ref, acc_ref, energy_ref, per)
    broaden(grid_ref, low_ref, fine, prof_ref, norm_ref, out_hbm, out_ref, out_sem)


def direct(abundances, sightline, pixel, counts, ion_table, doppler, lorentz_share):
    n_spec = lax.axis_size("spec")
    devices = lax.axis_size("los") * n_spec
    n_slots = abundances.shape[1]
    vmem = pl.BlockSpec(memory_space=pltpu.VMEM)
    smem = pl.BlockSpec(memory_space=pltpu.SMEM)
    anywhere = pl.BlockSpec(memory_space=pltpu.HBM)
    sent = pl.pallas_call(
        lambda *refs: pack_kernel(*refs, n_spec=n_spec),
        out_shape=jax.ShapeDtypeStruct((devices, LISTS * 8, 128), BF),
        in_specs=[anywhere] * 4,
        out_specs=anywhere,
        scratch_shapes=[
            pltpu.VMEM(abundances.shape, BF),
            pltpu.VMEM((n_slots // 128, 128), I32),
            pltpu.VMEM((n_slots // 128, 128), I32),
            pltpu.VMEM(counts.shape, I32),
            pltpu.VMEM((devices, LISTS * 8, 128), BF),
            pltpu.SemaphoreType.DMA((4,)),
            pltpu.SemaphoreType.DMA,
        ],
        compiler_params=pltpu.CompilerParams(vmem_limit_bytes=63 * 2**20),
        name="pack",
    )(abundances, sightline.reshape(n_slots // 128, 128), pixel.reshape(n_slots // 128, 128), counts)
    groups = LISTS * n_slots // GROUP
    n = BUCKETS * groups // LISTS
    table = jnp.pad(ion_table.T, ((0, 0), (0, VAL - ELEM)))
    prof, norm, left, scan, tri = pl.pallas_call(
        prepare_kernel,
        out_shape=[
            jax.ShapeDtypeStruct((ION, 2 * HW, 4 * HW), BF),
            jax.ShapeDtypeStruct((ION, 8, 2 * HW), F32),
            jax.ShapeDtypeStruct((OUTS, WIDE), BF),
            jax.ShapeDtypeStruct((9, 128, 128), BF),
            jax.ShapeDtypeStruct((GROUP, GROUP), BF),
        ],
        in_specs=[smem, smem, vmem],
        out_specs=[vmem] * 5,
        compiler_params=pltpu.CompilerParams(vmem_limit_bytes=10 * 2**20),
        cost_estimate=pl.CostEstimate(flops=20_000_000, bytes_accessed=4 * 2**20, transcendentals=3_000_000),
        name="prepare",
    )(doppler, lorentz_share, table)
    got = lax.all_to_all(sent, ("los", "spec"), split_axis=0, concat_axis=0, tiled=True)
    supers = LISTS * n_slots // SUPER + BUCKETS
    return pl.pallas_call(
        main_kernel,
        out_shape=[jax.ShapeDtypeStruct((ION, SL_DEV, PIX_DEV), F32), jax.ShapeDtypeStruct((1,), I32)],
        in_specs=[vmem] * 6,
        out_specs=[anywhere, smem],
        scratch_shapes=[
            pltpu.VMEM((groups, WIDE, GROUP), BF),
            pltpu.VMEM((groups, GROUP), F32),
            pltpu.VMEM((groups, GROUP), F32),
            pltpu.VMEM((groups, GROUP), F32),
            pltpu.VMEM((8, n), I32),
            pltpu.VMEM((groups * PITCH, WIDE), F32),
            pltpu.VMEM((supers * SUPER + STEP, WIDE), F32),
            pltpu.VMEM((supers, OUTS, SUPER), F32),
            pltpu.VMEM((ION, BUCKETS * PX, SL_DEV), BF),
            pltpu.VMEM((ION, BUCKETS * PX, SL_DEV), BF),
            pltpu.VMEM(((ION + 2) * PX, SL_DEV), F32),
            pltpu.VMEM((2, PX, SL_DEV), F32),
            pltpu.VMEM((ION, SL_DEV, PIX_DEV), F32),
            pltpu.SMEM((8, n), I32),
            pltpu.SemaphoreType.DMA,
            pltpu.SemaphoreType.DMA,
        ],
        compiler_params=pltpu.CompilerParams(vmem_limit_bytes=41 * 2**20),
        name="deposit_broaden",
    )(got, left, norm, scan, tri, prof)


def with_halo(cells, sides, width):
    for axis, dim in sides:
        count = lax.axis_size(axis)
        head = lax.slice_in_dim(cells, 0, width, axis=dim)
        tail = lax.slice_in_dim(cells, cells.shape[dim] - width, cells.shape[dim], axis=dim)
        cells = jnp.concatenate(
            [
                lax.ppermute(tail, axis, [(i, (i + 1) % count) for i in range(count)]),
                cells,
                lax.ppermute(head, axis, [((i + 1) % count, i) for i in range(count)]),
            ],
            axis=dim,
        )
    return cells


def line_shape(offset, doppler, share):
    u = offset / doppler
    return (1.0 - share) * jnp.exp(-u * u) + share / (1.0 + u * u)


def deposit_onto(got_cols, line_rows, place, span):
    ions = got_cols.shape[0]
    n_rows = got_cols.shape[1]
    pixel_hot = (place[:, None] == lax.broadcasted_iota(jnp.int32, (1, span), 1)).astype(
        jnp.bfloat16
    )
    line_hot = (line_rows[None, :] == lax.broadcasted_iota(jnp.int32, (SL_DEV, 1), 0)).astype(
        jnp.bfloat16
    )
    group = 8
    grouped = got_cols.reshape(ions // group, group, n_rows)

    def deposit(part_cols):
        spread = (part_cols[:, None, :] * line_hot[None, :, :]).reshape(group * SL_DEV, n_rows)
        return jnp.dot(spread, pixel_hot, preferred_element_type=jnp.float32).reshape(
            group, SL_DEV, span
        )

    return lax.map(deposit, grouped).reshape(ions, SL_DEV, span)


def broaden_window(padded, pix_dev, width, share, norm):
    inner = lax.broadcasted_iota(jnp.int32, (pix_dev + 2 * HW, pix_dev), 0)
    outer = lax.broadcasted_iota(jnp.int32, (pix_dev + 2 * HW, pix_dev), 1)
    delta = (outer + HW - inner).astype(jnp.float32)[None, :, :]
    matrix = jnp.where(jnp.abs(delta) <= HW, line_shape(delta, width, share), 0.0) / norm
    return jnp.einsum("isk,ikj->isj", padded, matrix, precision=lax.Precision.HIGHEST)


def general(abundances, sightline, pixel, counts, ion_table, doppler, lorentz_share):
    n_los = lax.axis_size("los")
    n_spec = lax.axis_size("spec")
    devices = n_los * n_spec
    n_slots = abundances.shape[1]
    slots = n_slots // devices
    pix_dev = PIXELS // n_spec
    columns = jnp.dot(ion_table.T, abundances.astype(jnp.float32), precision=lax.Precision.HIGHEST)
    live = lax.broadcasted_iota(jnp.int32, (devices, slots), 1) < counts[0][:, None]
    columns = jnp.where(live.reshape(1, n_slots), columns, 0.0).astype(jnp.bfloat16)
    cell = (sightline * pix_dev + pixel).reshape(1, n_slots)
    got_cols, got_cell = (
        lax.all_to_all(columns, ("los", "spec"), split_axis=1, concat_axis=1, tiled=True),
        lax.all_to_all(cell, ("los", "spec"), split_axis=1, concat_axis=1, tiled=True),
    )
    got_cell = got_cell.reshape(n_slots)
    grid = deposit_onto(got_cols, got_cell // pix_dev, got_cell % pix_dev, pix_dev)
    offsets = jnp.arange(-HW, HW + 1).astype(jnp.float32)
    totals = jnp.sum(line_shape(offsets[None, :], doppler[:, None], lorentz_share[:, None]), axis=1)
    width = doppler[:, None, None]
    share = lorentz_share[:, None, None]
    norm = totals[:, None, None]
    padded = with_halo(grid, (("spec", 2),), HW)
    depth = broaden_window(padded, pix_dev, width, share, norm)
    return depth


def on_device(*args):
    depth, again = direct(*args)
    return lax.fori_loop(0, again[0], lambda _, old: general(*args), depth)


def solution(mesh):
    in_specs = (
        P(None, ("los", "spec")),
        P(("los", "spec")),
        P(("los", "spec")),
        P(("los", "spec"), None),
        P(),
        P(),
        P(),
    )
    return jax.shard_map(
        on_device, mesh=mesh, in_specs=in_specs, out_specs=P(None, "los", "spec"), check_vma=False
    )
```
